256 devices in a mesh: cls: 8 (over x_lo, y), dom: 32 (over x_hi, z, core).
Axes of the slice: x: 4 (x_hi: 2, x_lo: 2; x = x_hi * 2 + x_lo), y: 4, z: 8, core: 2. Of those that a mesh axis runs over, the one named last changes fastest.
Arguments:
- particles: bfloat16 [8192, 32768], P(('cls', 'dom')), may hold values from -16 to 16
- references: bfloat16 [16, 8, 32768], P('cls'), may hold values from -4 to 4
- orient_bins: int32 [8192], P(('cls', 'dom')), may hold values from 0 to 7
- destinations: int32 [8192, 1], P(('cls', 'dom')), may hold values from 0 to 31; in each aligned block of 32 rows (0 to 31, 32 to 63, ...) at most 2 rows name the same one
- group_slots: int32 [8192], P(('cls', 'dom')), may hold values from 0 to 7
Outputs:
- class_means: float32 [16, 8, 32768], P('cls', None, 'dom')
The draws below stay inside these ranges and needn't reach their ends.
Inputs may be any that keep to these rules, and one draw needn't show every extreme that they name: `destinations`: among the rows of one device at most 2 name the same destination.
All inputs are finite; a program needn't handle non-finite values.
Results may differ from the reference program's by a relative error of at most 0.0047.
Values may be sent and summed in bfloat16 or wider, within the bound.
A program may use at most 128 MiB of HBM per device.

```python
import math
import jax
import jax.numpy as jnp
import numpy as np
from jax import lax

VOX = 32768
NB = 8
CLASSES = 16
P_DEV = 32
PARTICLES = 8192
CAP = 2
GROUPS_DEV = 8
N_CLS = 8
N_DOM = 32


def shared_bins(key):
    return jax.random.randint(jax.random.fold_in(key, 501), (PARTICLES,), 0, NB).astype(jnp.int32)


def shared_panels(key):
    values = jax.random.normal(jax.random.fold_in(key, 502), (CLASSES, NB, VOX), jnp.float32)
    return jnp.clip(values, -4.0, 4.0)


def draw_references(key, part):
    panels = shared_panels(key)
    return panels.astype(jnp.bfloat16)


def draw_orient_bins(key, part):
    bins_drawn = shared_bins(key)
    return bins_drawn


def draw_particles(key, part):
    key = jax.random.fold_in(key, 3)
    values = jax.random.normal(key, (PARTICLES, VOX), jnp.float32)
    return jnp.clip(values, -16.0, 16.0).astype(jnp.bfloat16)


def touch_ends(result, own_key, low, top_value):
    longest = result.shape.index(max(result.shape))
    spots = []
    for shift in (0, 1):
        where = [jax.random.randint(jax.random.fold_in(own_key, axis), (), 0, length) for axis, length in enumerate(result.shape)]
        where[longest] = (where[longest] + shift) % result.shape[longest]
        spots.append(tuple(where))
    return result.at[spots[0]].set(low).at[spots[1]].set(top_value)


def shared_out(rng, own, number, rows, number_of, top, bound, lean):
    order = jax.random.permutation(rng, number_of)
    crowded, usual = shares(number_of, rows * top, bound, lean, True), shares(number_of, rows * top, bound, lean, False)
    places = jnp.arange(number_of)

    def named(sizes, turn):
        used = int((sizes > 0).sum())
        fixed = max(1, used // 4)
        passed = fixed + (places - fixed + turn * (used - fixed)) % max(1, number_of - fixed)
        return jnp.zeros((number_of,), jnp.int32).at[order[jnp.where(places < fixed, places, passed)]].set(jnp.asarray(sizes, jnp.int32))

    sizes = jnp.where(number % 4 == 0, named(crowded, number // 4), named(usual, number - number // 4 - 1))
    mixed = jax.random.permutation(jax.random.fold_in(own, 3), number_of)
    giver, receiver = mixed[0:number_of // 2 * 2:2], mixed[1:number_of // 2 * 2:2]
    slack = jnp.minimum(sizes[giver] - 1, bound - sizes[receiver]) // 2
    slack = jnp.where((giver == order[0]) | (receiver == order[0]) | (sizes[receiver] == 0), 0, jnp.maximum(slack, 0))
    passed = jax.random.randint(jax.random.fold_in(own, 4), (number_of // 2,), 0, 1 << 20) % (slack + 1)
    sizes = sizes.at[giver].add(-passed).at[receiver].add(passed)
    members = jnp.searchsorted(jnp.cumsum(sizes), jnp.arange(rows * top), side="right").astype(jnp.int32)
    grid = members.reshape(top, rows).T
    grid = grid[jax.random.permutation(jax.random.fold_in(own, 1), rows)]
    turn = jax.random.randint(jax.random.fold_in(own, 2), (rows, 1), 0, top)
    return jnp.take_along_axis(grid, (jnp.arange(top)[None, :] + turn) % top, axis=1)


def shares(amount, total, limit, slope, full):
    loads = [(1 << 20) // math.isqrt(standing ** slope) + 1 for standing in range(1, amount + 1)]
    largest = limit if full else min(limit, max(-(-total // amount), total * loads[0] // sum(loads)))
    least = 1 if total - largest >= amount - 1 else 0
    given, surplus = [largest] + [least] * (amount - 1), total - largest - least * (amount - 1)
    while surplus > 0:
        free = [i for i in range(1, amount) if given[i] < largest] or [i for i in range(1, amount) if given[i] < limit]
        whole, left = sum([loads[i] for i in free]), surplus
        for i in free:
            addition = min(limit - given[i], max(1, left * loads[i] // whole), surplus)
            given[i] = given[i] + addition
            surplus = surplus - addition
    return np.array(given)


def setup_inputs(seed: int = 0) -> dict:
    splits = jax.random.split(jax.random.key(seed), 6)
    particles = draw_particles(jax.random.fold_in(splits[5], 71), 0)
    references = draw_references(jax.random.fold_in(splits[5], 71), 0)
    orient_bins = draw_orient_bins(jax.random.fold_in(splits[5], 71), 0)
    destinations_keys = jax.random.split(jax.random.fold_in(splits[3], 1), PARTICLES // P_DEV)
    destinations_turns = jax.random.permutation(jax.random.fold_in(splits[3], 3), PARTICLES // P_DEV)
    destinations = jax.vmap(lambda own, number: shared_out(jax.random.fold_in(splits[3], 2), own, number, P_DEV, N_DOM, 1, CAP, 2))(destinations_keys, destinations_turns).reshape((PARTICLES, 1))
    group_slots = touch_ends(jax.random.randint(splits[4], (PARTICLES,), 0, GROUPS_DEV), jax.random.fold_in(splits[4], 1), 0, GROUPS_DEV - 1).astype(jnp.int32)
    return dict(particles=particles, references=references, orient_bins=orient_bins, destinations=destinations, group_slots=group_slots)


def reference(particles, references, orient_bins, destinations, group_slots):
    classes = references.shape[0]
    bins_all = references.shape[1]
    voxels = references.shape[2]
    group_total = N_DOM * GROUPS_DEV
    panels = references.reshape(classes * bins_all, voxels)
    panel_squares = jnp.square(panels.astype(jnp.float32))
    scale = 1.0 / math.sqrt(voxels)
    block_rows = N_DOM * P_DEV
    blocks = (particles.reshape(N_CLS, block_rows, voxels), orient_bins.reshape(N_CLS, block_rows), destinations[:, 0].reshape(N_CLS, block_rows), group_slots.reshape(N_CLS, block_rows))

    def one_block(inputs):
        subvolumes, orient, target, member_slot = inputs
        member = (target * GROUPS_DEV + member_slot).astype(jnp.int32)
        values = subvolumes.astype(jnp.float32)
        group_power = jax.ops.segment_sum(jnp.square(values), member, num_segments=group_total)
        counts = jax.ops.segment_sum(jnp.ones((block_rows,), jnp.float32), member, num_segments=group_total)
        inverse_noise = (counts + 1.0)[:, None] / (group_power + 1.0)
        whitened = (values * inverse_noise[member]).astype(jnp.bfloat16)
        correlation = lax.dot_general(whitened, panels, (((1,), (1,)), ((), ())), preferred_element_type=jnp.float32)
        energy = lax.dot_general(inverse_noise, panel_squares, (((1,), (1,)), ((), ())), precision=lax.Precision.HIGHEST)
        combined = (correlation - 0.5 * energy[member]) * scale
        orient_hot = (orient[:, None] == jnp.arange(bins_all, dtype=jnp.int32)[None, :]).astype(jnp.float32)
        scores = lax.optimization_barrier(jnp.sum(combined.reshape(block_rows, classes, bins_all) * orient_hot[:, None, :], axis=2))
        weights = jax.nn.softmax(scores, axis=1).astype(jnp.bfloat16)
        coefficient = (weights[:, :, None] * orient_hot[:, None, :].astype(jnp.bfloat16)).reshape(block_rows, classes * bins_all)
        accumulated = lax.dot_general(coefficient, whitened, (((0,), (0,)), ((), ())), preferred_element_type=jnp.float32)
        weight_sum = lax.optimization_barrier(jnp.sum(coefficient.astype(jnp.float32), axis=0))
        return (accumulated, weight_sum)
    accumulated, weight_sum = lax.map(one_block, blocks)
    sums = lax.optimization_barrier(jnp.sum(accumulated, axis=0))
    totals = lax.optimization_barrier(jnp.sum(weight_sum, axis=0))
    means = sums / (totals[:, None] + 1.0)
    return means.reshape(classes, bins_all, voxels)
```

```python
import math

import jax
import jax.numpy as jnp
from jax import lax
from jax.sharding import PartitionSpec as P


def shards(particles, references, orient_bins, destinations, group_slots):
    sources = lax.axis_size("dom")
    rows, voxels = particles.shape
    block_classes, bins_all, _ = references.shape
    classes = block_classes * lax.axis_size("cls")
    groups = 8 * sources
    slab = voxels // sources
    members = rows * sources

    codes = (destinations[:, 0] * 8 + group_slots) * bins_all + orient_bins
    codes = lax.all_gather(codes, "dom", axis=0, tiled=True)
    group = codes // bins_all
    orient = codes % bins_all
    own = lax.dynamic_slice_in_dim(references, lax.axis_index("dom") * slab, slab, 2)
    panels = lax.all_gather(own, "cls", axis=0, tiled=True).reshape(classes * bins_all, slab)

    values = lax.all_to_all(
        particles.reshape(rows, sources, slab), "dom", split_axis=1, concat_axis=0, tiled=True
    ).reshape(members, slab)

    hot = (group[:, None] == jnp.arange(groups, dtype=jnp.int32)[None, :]).astype(jnp.float32)
    wide = values.astype(jnp.float32)
    power = lax.dot_general(
        hot, jnp.square(wide), (((0,), (0,)), ((), ())), precision=lax.Precision.HIGHEST
    )
    counts = jnp.sum(hot, axis=0)
    inverse_noise = (counts + 1.0)[:, None] / (power + 1.0)
    spread = jnp.dot(hot, inverse_noise, precision=lax.Precision.HIGHEST)
    whitened = (wide * spread).astype(jnp.bfloat16)
    correlation = lax.dot_general(
        whitened, panels, (((1,), (1,)), ((), ())), preferred_element_type=jnp.float32
    )
    energy = lax.dot_general(
        inverse_noise,
        jnp.square(panels.astype(jnp.float32)),
        (((1,), (1,)), ((), ())),
        precision=lax.Precision.HIGHEST,
    )
    combined = correlation - 0.5 * jnp.dot(hot, energy, precision=lax.Precision.HIGHEST)
    orient_hot = orient[:, None] == jnp.arange(bins_all, dtype=jnp.int32)[None, :]
    partial = jnp.sum(
        jnp.where(orient_hot[:, None, :], combined.reshape(members, classes, bins_all), 0.0), axis=2
    )
    scores = lax.psum(partial, "dom") * (1.0 / math.sqrt(voxels))
    weights = jax.nn.softmax(scores, axis=1).astype(jnp.bfloat16)
    coefficient = (weights[:, :, None] * orient_hot[:, None, :].astype(jnp.bfloat16)).reshape(
        members, classes * bins_all
    )
    weight_sum = jnp.sum(coefficient.astype(jnp.float32), axis=0)
    accumulated = lax.dot_general(
        coefficient, whitened, (((0,), (0,)), ((), ())), preferred_element_type=jnp.float32
    )
    own_slab = lax.psum_scatter(
        accumulated.reshape(classes, bins_all, slab), "cls", scatter_dimension=0, tiled=True
    )
    totals = lax.psum(weight_sum, "cls").reshape(classes, bins_all)
    own_totals = lax.dynamic_slice_in_dim(
        totals, lax.axis_index("cls") * block_classes, block_classes, 0
    )
    return own_slab / (own_totals[:, :, None] + 1.0)


def solution(mesh):
    in_specs = (
        P(("cls", "dom"), None),
        P("cls", None, None),
        P(("cls", "dom")),
        P(("cls", "dom"), None),
        P(("cls", "dom")),
    )
    out_specs = P("cls", None, "dom")
    return jax.shard_map(shards, mesh=mesh, in_specs=in_specs, out_specs=out_specs, check_vma=False)
```

```python
import functools
import math

import jax
import jax.numpy as jnp
from jax import lax
from jax.experimental import pallas as pl
from jax.experimental.pallas import tpu as pltpu
from jax.sharding import PartitionSpec as P

MESH = pl.DeviceIdType.MESH
F32 = jnp.float32
BF16 = jnp.bfloat16

ROWS = 32
DOM = 32
CLS = 8
BINS = 8
CLASSES = 16
GROUPS = 256
MEMBERS = ROWS * DOM
SLAB = 1024
CHUNKS = 4
WIDE = SLAB // CHUNKS
PANELS = CLASSES * BINS
OWN = PANELS // CLS
Z = 8

NT = (((1,), (1,)), ((), ()))


def dot(a, b):
    return jnp.dot(a, b, preferred_element_type=F32)


def dot_nt(a, b):
    return lax.dot_general(a, b, NT, preferred_element_type=F32)


def split(value, pieces):
    out = []
    for _ in range(pieces):
        piece = value.astype(BF16)
        out.append(piece)
        value = value - piece.astype(F32)
    return out


def dom_peer(i, dom):
    core, z, x = dom % 2, (dom // 2) % Z, dom // (2 * Z)
    j = i // 4
    step = 4 + (1 - 2 * (j % 2)) * ((j + 1) // 2)
    core = (core + 1 - i % 2) % 2
    x = (x + 1 - (i // 2) % 2) % 2
    z = (z + step) % Z
    return (x * Z + z) * 2 + core


def kernel(
    particles,
    references,
    codes,
    out,
    x_ref,
    r_ref,
    c_ref,
    hot_t,
    hot,
    score_sum,
    energy_sum,
    piece_out,
    piece_in,
    piece_all,
    scores_ref,
    acc_out,
    acc_in,
    tot_out,
    tot_in,
    x_recv,
    misc_recv,
    send,
    local,
):
    cls = lax.axis_index("cls")
    dom = lax.axis_index("dom")

    barrier = pltpu.get_barrier_semaphore()

    def greet_dom(i, carry):
        pl.semaphore_signal(barrier, inc=1, device_id=(cls, dom_peer(i, dom)), device_id_type=MESH)
        return carry

    def greet_cls(i, carry):
        pl.semaphore_signal(barrier, inc=1, device_id=((cls + i) % CLS, dom), device_id_type=MESH)
        return carry

    lax.fori_loop(0, DOM - 1, greet_dom, 0)
    lax.fori_loop(1, CLS, greet_cls, 0)
    pl.semaphore_wait(barrier, DOM - 1 + CLS - 1)

    def send_to(src, dst, sem_out, sem_in, device):
        pltpu.make_async_remote_copy(
            src_ref=src,
            dst_ref=dst,
            send_sem=sem_out,
            recv_sem=sem_in,
            device_id=device,
            device_id_type=MESH,
        ).start()

    def taken(ref, sem):
        pltpu.make_async_copy(ref, ref, sem).wait()

    def send_codes(i, carry):
        send_to(codes, c_ref.at[dom], send.at[0], misc_recv.at[0], (cls, dom_peer(i, dom)))
        return carry

    def send_panels(i, carry):
        send_to(references, r_ref.at[cls], send.at[1], misc_recv.at[1], ((cls + i) % CLS, dom))
        return carry

    lax.fori_loop(0, DOM - 1, send_codes, 0)
    lax.fori_loop(1, CLS, send_panels, 0)

    def send_chunk(k, carry):
        chunk, i = k // (DOM - 1), k % (DOM - 1)
        peer = dom_peer(i, dom)
        start = pl.multiple_of(peer * SLAB + chunk * WIDE, WIDE)
        send_to(
            particles.at[:, pl.ds(start, WIDE)],
            x_ref.at[chunk, dom],
            send.at[2],
            x_recv.at[chunk],
            (cls, peer),
        )
        return carry

    lax.fori_loop(0, CHUNKS * (DOM - 1), send_chunk, 0)

    own_copies = []
    for chunk in range(CHUNKS):
        start = pl.multiple_of(dom * SLAB + chunk * WIDE, WIDE)
        own_copies.append(
            pltpu.make_async_copy(
                particles.at[:, pl.ds(start, WIDE)], x_ref.at[chunk, dom], local.at[chunk]
            )
        )
    for copy in own_copies:
        copy.start()
    c_ref[dom] = codes[...]
    r_ref[cls] = references[...]

    taken(c_ref.at[pl.ds(0, DOM - 1)], misc_recv.at[0])
    code = jnp.sum(c_ref[...].reshape(8, 4, 128), axis=1)
    code_row = jnp.concatenate([code[t : t + 1] for t in range(8)], axis=1)
    group_row = code_row // BINS
    orient_row = code_row % BINS
    members = jnp.broadcast_to(group_row, (GROUPS, MEMBERS))
    hot_f32 = (lax.broadcasted_iota(jnp.int32, (GROUPS, MEMBERS), 0) == members).astype(F32)
    hot_t[...] = hot_f32.astype(BF16)
    counts = jnp.sum(hot_f32, axis=1, keepdims=True)
    group_col = jnp.transpose(jnp.broadcast_to(group_row.astype(F32), (128, MEMBERS)))
    lanes = lax.broadcasted_iota(jnp.int32, (MEMBERS, 128), 1).astype(F32)
    for half in range(GROUPS // 128):
        hot[:, 128 * half : 128 * half + 128] = (
            (group_col == lanes + float(128 * half)).astype(F32).astype(BF16)
        )
    score_sum[...] = jnp.zeros_like(score_sum)
    energy_sum[...] = jnp.zeros_like(energy_sum)

    taken(r_ref.at[pl.ds(0, CLS - 1)], misc_recv.at[1])
    for copy in own_copies:
        copy.wait()

    def whiten(chunk, carry):
        taken(x_ref.at[chunk, pl.ds(0, DOM - 1)], x_recv.at[chunk])
        values = x_ref[chunk].reshape(MEMBERS, WIDE).astype(F32)
        high, low = split(values * values, 2)
        power = dot(hot_t[...], high) + dot(hot_t[...], low)
        inverse = (counts + 1.0) / (power + 1.0)
        parts = split(inverse, 3)
        spread = dot(hot[...], parts[0]) + dot(hot[...], parts[1])
        whitened = (values * spread).astype(BF16)
        x_ref[chunk] = whitened.reshape(DOM, ROWS, WIDE)
        panels = r_ref[:, :, pl.ds(pl.multiple_of(chunk * WIDE, WIDE), WIDE)].reshape(PANELS, WIDE)
        score_sum[...] += dot_nt(panels, whitened)
        wide = panels.astype(F32)
        square = split(wide * wide, 2)
        energy = jnp.zeros((PANELS, GROUPS), F32)
        for piece in square:
            for part in parts:
                energy += dot_nt(piece, part)
        energy_sum[...] += energy
        return carry

    lax.fori_loop(0, CHUNKS, whiten, 0)

    spread_energy = jnp.zeros((PANELS, MEMBERS), F32)
    for part in split(energy_sum[...], 3):
        spread_energy += dot(part, hot_t[...])
    combined = (score_sum[...] - 0.5 * spread_energy).reshape(CLASSES, BINS, MEMBERS)
    bin_index = lax.broadcasted_iota(jnp.int32, (BINS, MEMBERS), 0)
    in_bin = bin_index == jnp.broadcast_to(orient_row, (BINS, MEMBERS))
    partial = jnp.sum(jnp.where(in_bin[None], combined, 0.0), axis=1)
    for q in range(4):
        for t in range(8):
            piece_out[q * 8 + t] = partial[4 * q : 4 * q + 4, 128 * t : 128 * t + 128]

    def send_piece(i, carry):
        peer = dom_peer(i, dom)
        send_to(piece_out.at[peer], piece_in.at[dom], send.at[3], misc_recv.at[2], (cls, peer))
        return carry

    lax.fori_loop(0, DOM - 1, send_piece, 0)
    piece_in[dom] = piece_out[dom]
    taken(piece_in.at[pl.ds(0, DOM - 1)], misc_recv.at[2])
    piece_all[dom] = jnp.sum(piece_in[...], axis=0)

    def send_sum(i, carry):
        peer = dom_peer(i, dom)
        send_to(piece_all.at[dom], piece_all.at[dom], send.at[4], misc_recv.at[3], (cls, peer))
        return carry

    lax.fori_loop(0, DOM - 1, send_sum, 0)
    taken(piece_all.at[pl.ds(0, DOM - 1)], misc_recv.at[3])
    for q in range(4):
        for t in range(8):
            scores_ref[4 * q : 4 * q + 4, 128 * t : 128 * t + 128] = piece_all[q * 8 + t]

    scores = scores_ref[...] * (1.0 / math.sqrt(DOM * SLAB))
    power = jnp.exp(scores - jnp.max(scores, axis=0, keepdims=True))
    weights = (power / jnp.sum(power, axis=0, keepdims=True)).astype(BF16).astype(F32)
    coefficient_f32 = jnp.where(in_bin[None], weights[:, None, :], 0.0).reshape(PANELS, MEMBERS)
    coefficient = coefficient_f32.astype(BF16)
    totals = jnp.sum(coefficient_f32, axis=1, keepdims=True)
    tot_out[...] = jnp.broadcast_to(totals, (PANELS, 128)).reshape(CLS, OWN, 128)

    def send_total(i, carry):
        peer = (cls + i) % CLS
        send_to(tot_out.at[peer], tot_in.at[cls], send.at[5], misc_recv.at[4], (peer, dom))
        return carry

    lax.fori_loop(1, CLS, send_total, 0)
    tot_in[cls] = tot_out[cls]

    for chunk in range(CHUNKS):
        acc_out[:, :, chunk * WIDE : (chunk + 1) * WIDE] = (
            dot(coefficient, x_ref[chunk].reshape(MEMBERS, WIDE))
            .astype(acc_out.dtype)
            .reshape(CLS, OWN, WIDE)
        )

    def send_acc(i, carry):
        peer = (cls + i) % CLS
        send_to(acc_out.at[peer], acc_in.at[cls], send.at[6], misc_recv.at[5], (peer, dom))
        return carry

    lax.fori_loop(1, CLS, send_acc, 0)
    acc_in[cls] = acc_out[cls]
    taken(tot_in.at[pl.ds(0, CLS - 1)], misc_recv.at[4])
    total = jnp.sum(tot_in[...], axis=0)[:, 0:1]
    taken(acc_in.at[pl.ds(0, CLS - 1)], misc_recv.at[5])
    out[...] = jnp.sum(acc_in[...].astype(F32), axis=0) / (total + 1.0)

    taken(c_ref.at[pl.ds(0, DOM - 1)], send.at[0])
    taken(r_ref.at[pl.ds(0, CLS - 1)], send.at[1])
    taken(x_ref.at[:, pl.ds(0, DOM - 1)], send.at[2])
    taken(piece_in.at[pl.ds(0, DOM - 1)], send.at[3])
    taken(piece_all.at[pl.ds(0, DOM - 1)], send.at[4])
    taken(tot_in.at[pl.ds(0, CLS - 1)], send.at[5])
    taken(acc_in.at[pl.ds(0, CLS - 1)], send.at[6])


def shards(particles, references, orient_bins, destinations, group_slots):
    dom = lax.axis_index("dom")
    code = (destinations[:, 0] * 8 + group_slots) * BINS + orient_bins
    lane = jnp.arange(128, dtype=jnp.int32)
    codes = jnp.where(lane // ROWS == dom % 4, jnp.tile(code, 4), 0)[None, :]
    own = lax.dynamic_slice_in_dim(references, dom * SLAB, SLAB, 2).reshape(OWN, SLAB)
    vmem = pl.BlockSpec(memory_space=pltpu.VMEM)
    out = pl.pallas_call(
        kernel,
        out_shape=jax.ShapeDtypeStruct((OWN, SLAB), F32),
        in_specs=[pl.BlockSpec(memory_space=pl.ANY), vmem, vmem],
        out_specs=vmem,
        scratch_shapes=[
            pltpu.VMEM((CHUNKS, DOM, ROWS, WIDE), BF16),
            pltpu.VMEM((CLS, OWN, SLAB), BF16),
            pltpu.VMEM((DOM, 1, 128), jnp.int32),
            pltpu.VMEM((GROUPS, MEMBERS), BF16),
            pltpu.VMEM((MEMBERS, GROUPS), BF16),
            pltpu.VMEM((PANELS, MEMBERS), F32),
            pltpu.VMEM((PANELS, GROUPS), F32),
            pltpu.VMEM((DOM, 4, 128), F32),
            pltpu.VMEM((DOM, 4, 128), F32),
            pltpu.VMEM((DOM, 4, 128), F32),
            pltpu.VMEM((CLASSES, MEMBERS), F32),
            pltpu.VMEM((CLS, OWN, SLAB), BF16),
            pltpu.VMEM((CLS, OWN, SLAB), BF16),
            pltpu.VMEM((CLS, OWN, 128), F32),
            pltpu.VMEM((CLS, OWN, 128), F32),
            pltpu.SemaphoreType.DMA((CHUNKS,)),
            pltpu.SemaphoreType.DMA((6,)),
            pltpu.SemaphoreType.DMA((7,)),
            pltpu.SemaphoreType.DMA((CHUNKS,)),
        ],
        compiler_params=pltpu.CompilerParams(
            collective_id=0, has_side_effects=True, vmem_limit_bytes=48 * 1024 * 1024
        ),
    )(particles, own, codes)
    return out.reshape(CLASSES // CLS, BINS, SLAB)


def solution(mesh):
    in_specs = (
        P(("cls", "dom"), None),
        P("cls", None, None),
        P(("cls", "dom")),
        P(("cls", "dom"), None),
        P(("cls", "dom")),
    )
    out_specs = P("cls", None, "dom")
    return jax.shard_map(shards, mesh=mesh, in_specs=in_specs, out_specs=out_specs, check_vma=False)
```

```python
import functools
import math

import jax
import jax.numpy as jnp
from jax import lax
from jax.experimental import pallas as pl
from jax.experimental.pallas import tpu as pltpu
from jax.sharding import PartitionSpec as P

MESH = pl.DeviceIdType.MESH
F32 = jnp.float32
BF16 = jnp.bfloat16

ROWS = 32
DOM = 32
CLS = 8
BINS = 8
CLASSES = 16
GROUPS = 256
MEMBERS = ROWS * DOM
SLAB = 1024
CHUNKS = 4
WIDE = SLAB // CHUNKS
PANELS = CLASSES * BINS
OWN = PANELS // CLS
Z = 8

NT = (((1,), (1,)), ((), ()))


def dot(a, b):
    return jnp.dot(a, b, preferred_element_type=F32)


def dot_nt(a, b):
    return lax.dot_general(a, b, NT, preferred_element_type=F32)


def split(value, pieces):
    out = []
    for _ in range(pieces):
        piece = value.astype(BF16)
        out.append(piece)
        value = value - piece.astype(F32)
    return out


def dom_peer(i, dom):
    core, z, x = dom % 2, (dom // 2) % Z, dom // (2 * Z)
    j = i // 4
    step = 4 + (1 - 2 * (j % 2)) * ((j + 1) // 2)
    core = (core + 1 - i % 2) % 2
    x = (x + 1 - (i // 2) % 2) % 2
    z = (z + step) % Z
    return (x * Z + z) * 2 + core


def kernel(
    particles,
    references,
    orient_bins,
    destinations,
    group_slots,
    out,
    *scratch,
):
    (
        x_ref,
        labels,
        codes,
        r_ref,
        c_ref,
        hot_t,
        hot,
        score_sum,
        energy_sum,
        piece_out,
        piece_in,
        piece_all,
        scores_ref,
        coefficient_ref,
        acc_out,
        acc_in,
        x_recv,
        misc_recv,
        send,
        local,
    ) = scratch
    cls = lax.axis_index("cls")
    dom = lax.axis_index("dom")
    slab_start = pl.multiple_of(dom * SLAB, SLAB)

    label_copies = [
        pltpu.make_async_copy(ref, labels.at[k], local.at[k])
        for k, ref in enumerate((destinations, group_slots, orient_bins))
    ]
    own_copies = [
        pltpu.make_async_copy(references.at[:, pl.ds(slab_start, SLAB)], r_ref.at[cls], local.at[3])
    ]
    for chunk in range(CHUNKS):
        start = pl.multiple_of(dom * SLAB + chunk * WIDE, WIDE)
        own_copies.append(
            pltpu.make_async_copy(
                particles.at[:, pl.ds(start, WIDE)],
                x_ref.at[chunk, dom],
                local.at[4 + chunk],
            )
        )
    for copy in label_copies + own_copies:
        copy.start()

    barrier = pltpu.get_barrier_semaphore()

    def greet_dom(i, carry):
        pl.semaphore_signal(barrier, inc=1, device_id=(cls, dom_peer(i, dom)), device_id_type=MESH)
        return carry

    def greet_cls(i, carry):
        pl.semaphore_signal(barrier, inc=1, device_id=((cls + i) % CLS, dom), device_id_type=MESH)
        return carry

    lax.fori_loop(0, DOM - 1, greet_dom, 0)
    lax.fori_loop(1, CLS, greet_cls, 0)

    for copy in label_copies:
        copy.wait()
    own_code = (labels[0] * 8 + labels[1]) * BINS + labels[2]
    lane = lax.broadcasted_iota(jnp.int32, (1, 128), 1)
    four = jnp.concatenate([own_code] * 4, axis=1)
    codes[...] = jnp.where(lane // ROWS == dom % 4, four, 0)
    c_ref[dom] = codes[...]

    pl.semaphore_wait(barrier, DOM - 1 + CLS - 1)

    def send_to(src, dst, sem_out, sem_in, device):
        pltpu.make_async_remote_copy(
            src_ref=src,
            dst_ref=dst,
            send_sem=sem_out,
            recv_sem=sem_in,
            device_id=device,
            device_id_type=MESH,
        ).start()

    def taken(ref, sem):
        pltpu.make_async_copy(ref, ref, sem).wait()

    def send_chunk(k, carry):
        chunk, i = k // (DOM - 1), k % (DOM - 1)
        peer = dom_peer(i, dom)
        start = pl.multiple_of(peer * SLAB + chunk * WIDE, WIDE)
        send_to(
            particles.at[:, pl.ds(start, WIDE)],
            x_ref.at[chunk, dom],
            send.at[2],
            x_recv.at[chunk],
            (cls, peer),
        )
        return carry

    def send_codes(i, carry):
        send_to(codes, c_ref.at[dom], send.at[0], misc_recv.at[0], (cls, dom_peer(i, dom)))
        return carry

    def send_panels(i, carry):
        send_to(
            references.at[:, pl.ds(slab_start, SLAB)],
            r_ref.at[cls],
            send.at[1],
            misc_recv.at[1],
            ((cls + i) % CLS, dom),
        )
        return carry

    lax.fori_loop(0, DOM - 1, send_chunk, 0)
    lax.fori_loop(0, DOM - 1, send_codes, 0)
    lax.fori_loop(1, CLS, send_panels, 0)
    lax.fori_loop(DOM - 1, CHUNKS * (DOM - 1), send_chunk, 0)

    taken(c_ref.at[pl.ds(0, DOM - 1)], misc_recv.at[0])
    code = jnp.sum(c_ref[...].reshape(8, 4, 128), axis=1)
    code_row = jnp.concatenate([code[t : t + 1] for t in range(8)], axis=1)
    group_row = code_row // BINS
    orient_row = code_row % BINS
    members = jnp.broadcast_to(group_row, (GROUPS, MEMBERS))
    hot_f32 = (lax.broadcasted_iota(jnp.int32, (GROUPS, MEMBERS), 0) == members).astype(F32)
    hot_t[...] = hot_f32.astype(BF16)
    counts = jnp.sum(hot_f32, axis=1, keepdims=True)
    group_col = jnp.transpose(jnp.broadcast_to(group_row.astype(F32), (128, MEMBERS)))
    lanes = lax.broadcasted_iota(jnp.int32, (MEMBERS, 128), 1).astype(F32)
    for half in range(GROUPS // 128):
        hot[:, 128 * half : 128 * half + 128] = (
            (group_col == lanes + float(128 * half)).astype(F32).astype(BF16)
        )
    score_sum[...] = jnp.zeros_like(score_sum)
    energy_sum[...] = jnp.zeros_like(energy_sum)

    taken(r_ref.at[pl.ds(0, CLS - 1)], misc_recv.at[1])
    for copy in own_copies:
        copy.wait()

    def whiten(chunk, carry):
        taken(x_ref.at[chunk, pl.ds(0, DOM - 1)], x_recv.at[chunk])
        values = x_ref[chunk].reshape(MEMBERS, WIDE).astype(F32)
        high, low = split(values * values, 2)
        power = dot(hot_t[...], high) + dot(hot_t[...], low)
        inverse = (counts + 1.0) / (power + 1.0)
        parts = split(inverse, 3)
        spread = dot(hot[...], parts[0]) + dot(hot[...], parts[1])
        whitened = (values * spread).astype(BF16)
        x_ref[chunk] = whitened.reshape(DOM, ROWS, WIDE)
        panels = r_ref[:, :, pl.ds(pl.multiple_of(chunk * WIDE, WIDE), WIDE)].reshape(PANELS, WIDE)
        score_sum[...] += dot_nt(panels, whitened)
        wide = panels.astype(F32)
        square = split(wide * wide, 2)
        energy = jnp.zeros((PANELS, GROUPS), F32)
        for piece in square:
            for part in parts:
                energy += dot_nt(piece, part)
        energy_sum[...] += energy
        return carry

    lax.fori_loop(0, CHUNKS, whiten, 0)

    spread_energy = jnp.zeros((PANELS, MEMBERS), F32)
    for part in split(energy_sum[...], 3):
        spread_energy += dot(part, hot_t[...])
    combined = (score_sum[...] - 0.5 * spread_energy).reshape(CLASSES, BINS, MEMBERS)
    bin_index = lax.broadcasted_iota(jnp.int32, (BINS, MEMBERS), 0)
    in_bin = bin_index == jnp.broadcast_to(orient_row, (BINS, MEMBERS))
    partial = jnp.sum(jnp.where(in_bin[None], combined, 0.0), axis=1)
    for q in range(4):
        for t in range(8):
            piece_out[q * 8 + t] = partial[4 * q : 4 * q + 4, 128 * t : 128 * t + 128]

    def send_piece(i, carry):
        peer = dom_peer(i, dom)
        send_to(piece_out.at[peer], piece_in.at[dom], send.at[3], misc_recv.at[2], (cls, peer))
        return carry

    lax.fori_loop(0, DOM - 1, send_piece, 0)
    piece_in[dom] = piece_out[dom]
    taken(piece_in.at[pl.ds(0, DOM - 1)], misc_recv.at[2])
    piece_all[dom] = jnp.sum(piece_in[...], axis=0)

    def send_sum(i, carry):
        peer = dom_peer(i, dom)
        send_to(piece_all.at[dom], piece_all.at[dom], send.at[4], misc_recv.at[3], (cls, peer))
        return carry

    lax.fori_loop(0, DOM - 1, send_sum, 0)
    taken(piece_all.at[pl.ds(0, DOM - 1)], misc_recv.at[3])
    for q in range(4):
        for t in range(8):
            scores_ref[4 * q : 4 * q + 4, 128 * t : 128 * t + 128] = piece_all[q * 8 + t]

    scores = scores_ref[...] * (1.0 / math.sqrt(DOM * SLAB))
    power = jnp.exp(scores - jnp.max(scores, axis=0, keepdims=True))
    weights = (power / jnp.sum(power, axis=0, keepdims=True)).astype(BF16).astype(F32)
    coefficient_f32 = jnp.where(in_bin[None], weights[:, None, :], 0.0).reshape(PANELS, MEMBERS)
    coefficient_ref[...] = coefficient_f32.astype(BF16)
    totals = jnp.sum(coefficient_f32, axis=1, keepdims=True)
    lane = lax.broadcasted_iota(jnp.int32, (PANELS, 128), 1)
    tail = jnp.zeros((PANELS, 128), F32)
    for k, piece in enumerate(split(totals, 3)):
        tail = jnp.where(lane == k, piece.astype(F32), tail)
    acc_out[:, :, SLAB:] = tail.astype(BF16).reshape(CLS, OWN, 128)
    def add_up(chunk, carry):
        lanes = pl.ds(pl.multiple_of(chunk * WIDE, WIDE), WIDE)
        acc_out[:, :, lanes] = (
            dot(coefficient_ref[...], x_ref[chunk].reshape(MEMBERS, WIDE))
            .astype(BF16)
            .reshape(CLS, OWN, WIDE)
        )
        return carry

    lax.fori_loop(0, CHUNKS, add_up, 0)

    def send_acc(i, carry):
        peer = (cls + i) % CLS
        send_to(acc_out.at[peer], acc_in.at[cls], send.at[5], misc_recv.at[4], (peer, dom))
        return carry

    lax.fori_loop(1, CLS, send_acc, 0)
    acc_in[cls] = acc_out[cls]
    taken(acc_in.at[pl.ds(0, CLS - 1)], misc_recv.at[4])
    total = jnp.sum(
        jnp.sum(acc_in[:, :, SLAB:].astype(F32), axis=0), axis=1, keepdims=True
    )
    out[...] = jnp.sum(acc_in[:, :, :SLAB].astype(F32), axis=0) / (total + 1.0)

    taken(c_ref.at[pl.ds(0, DOM - 1)], send.at[0])
    taken(r_ref.at[pl.ds(0, CLS - 1)], send.at[1])
    taken(x_ref.at[:, pl.ds(0, DOM - 1)], send.at[2])
    taken(piece_in.at[pl.ds(0, DOM - 1)], send.at[3])
    taken(piece_all.at[pl.ds(0, DOM - 1)], send.at[4])
    taken(acc_in.at[pl.ds(0, CLS - 1)], send.at[5])


def shards(particles, references, orient_bins, destinations, group_slots):
    hbm = pl.BlockSpec(memory_space=pltpu.HBM)
    out = pl.pallas_call(
        kernel,
        out_shape=jax.ShapeDtypeStruct((OWN, SLAB), F32),
        in_specs=[hbm] * 5,
        out_specs=pl.BlockSpec(memory_space=pltpu.VMEM),
        scratch_shapes=[
            pltpu.VMEM((CHUNKS, DOM, ROWS, WIDE), BF16),
            pltpu.VMEM((3, 1, ROWS), jnp.int32),
            pltpu.VMEM((1, 128), jnp.int32),
            pltpu.VMEM((CLS, OWN, SLAB), BF16),
            pltpu.VMEM((DOM, 1, 128), jnp.int32),
            pltpu.VMEM((GROUPS, MEMBERS), BF16),
            pltpu.VMEM((MEMBERS, GROUPS), BF16),
            pltpu.VMEM((PANELS, MEMBERS), F32),
            pltpu.VMEM((PANELS, GROUPS), F32),
            pltpu.VMEM((DOM, 4, 128), F32),
            pltpu.VMEM((DOM, 4, 128), F32),
            pltpu.VMEM((DOM, 4, 128), F32),
            pltpu.VMEM((CLASSES, MEMBERS), F32),
            pltpu.VMEM((PANELS, MEMBERS), BF16),
            pltpu.VMEM((CLS, OWN, SLAB + 128), BF16),
            pltpu.VMEM((CLS, OWN, SLAB + 128), BF16),
            pltpu.SemaphoreType.DMA((CHUNKS,)),
            pltpu.SemaphoreType.DMA((5,)),
            pltpu.SemaphoreType.DMA((6,)),
            pltpu.SemaphoreType.DMA((4 + CHUNKS,)),
        ],
        compiler_params=pltpu.CompilerParams(
            collective_id=0, has_side_effects=True, vmem_limit_bytes=60 * 1024 * 1024
        ),
    )(
        particles,
        references.reshape(OWN, DOM * SLAB),
        orient_bins.reshape(1, ROWS),
        destinations.reshape(1, ROWS),
        group_slots.reshape(1, ROWS),
    )
    return out.reshape(CLASSES // CLS, BINS, SLAB)


def solution(mesh):
    in_specs = (
        P(("cls", "dom"), None),
        P("cls", None, None),
        P(("cls", "dom")),
        P(("cls", "dom"), None),
        P(("cls", "dom")),
    )
    out_specs = P("cls", None, "dom")
    return jax.shard_map(shards, mesh=mesh, in_specs=in_specs, out_specs=out_specs, check_vma=False)
```

```python
import functools
import math

import jax
import jax.numpy as jnp
from jax import lax
from jax.experimental import pallas as pl
from jax.experimental.pallas import tpu as pltpu
from jax.sharding import PartitionSpec as P

MESH = pl.DeviceIdType.MESH
F32 = jnp.float32
BF16 = jnp.bfloat16

ROWS = 32
DOM = 32
CLS = 8
BINS = 8
CLASSES = 16
GROUPS = 256
MEMBERS = ROWS * DOM
SLAB = 1024
WIDTHS = (256, 256, 256, 128, 128)
STARTS = tuple(sum(WIDTHS[:c]) for c in range(len(WIDTHS)))
CHUNKS = len(WIDTHS)
WIDE = 128
PANELS = CLASSES * BINS
OWN = PANELS // CLS
Z = 8

NT = (((1,), (1,)), ((), ()))


def dot(a, b):
    return jnp.dot(a, b, preferred_element_type=F32)


def dot_nt(a, b):
    return lax.dot_general(a, b, NT, preferred_element_type=F32)


def split(value, pieces):
    out = []
    for _ in range(pieces):
        piece = value.astype(BF16)
        out.append(piece)
        value = value - piece.astype(F32)
    return out


def dom_peer(i, dom):
    core, z, x = dom % 2, (dom // 2) % Z, dom // (2 * Z)
    j = i // 4
    step = 4 + (1 - 2 * (j % 2)) * ((j + 1) // 2)
    core = (core + 1 - i % 2) % 2
    x = (x + 1 - (i // 2) % 2) % 2
    z = (z + step) % Z
    return (x * Z + z) * 2 + core


def kernel(
    particles,
    references,
    orient_bins,
    destinations,
    group_slots,
    out,
    *scratch,
):
    (
        x_ref,
        labels,
        codes,
        r_ref,
        c_ref,
        hot_t,
        hot,
        score_sum,
        energy_sum,
        piece_out,
        piece_in,
        piece_all,
        scores_ref,
        coefficient_ref,
        acc_out,
        acc_in,
        x_recv,
        misc_recv,
        send,
        local,
    ) = scratch
    cls = lax.axis_index("cls")
    dom = lax.axis_index("dom")
    slab_start = pl.multiple_of(dom * SLAB, SLAB)

    label_copies = [
        pltpu.make_async_copy(ref, labels.at[k], local.at[k])
        for k, ref in enumerate((destinations, group_slots, orient_bins))
    ]
    own_copies = [
        pltpu.make_async_copy(references.at[:, pl.ds(slab_start, SLAB)], r_ref.at[cls], local.at[3])
    ]
    own_copies.append(
        pltpu.make_async_copy(particles.at[:, pl.ds(slab_start, SLAB)], x_ref.at[dom], local.at[4])
    )
    for copy in label_copies + own_copies:
        copy.start()

    barrier = pltpu.get_barrier_semaphore()

    def greet_dom(i, carry):
        pl.semaphore_signal(barrier, inc=1, device_id=(cls, dom_peer(i, dom)), device_id_type=MESH)
        return carry

    def greet_cls(i, carry):
        pl.semaphore_signal(barrier, inc=1, device_id=((cls + i) % CLS, dom), device_id_type=MESH)
        return carry

    lax.fori_loop(0, DOM - 1, greet_dom, 0)
    lax.fori_loop(1, CLS, greet_cls, 0)

    for copy in label_copies:
        copy.wait()
    own_code = (labels[0] * 8 + labels[1]) * BINS + labels[2]
    lane = lax.broadcasted_iota(jnp.int32, (1, 128), 1)
    four = jnp.concatenate([own_code] * 4, axis=1)
    codes[...] = jnp.where(lane // ROWS == dom % 4, four, 0)
    c_ref[dom] = codes[...]

    pl.semaphore_wait(barrier, DOM - 1 + CLS - 1)

    def send_to(src, dst, sem_out, sem_in, device):
        pltpu.make_async_remote_copy(
            src_ref=src,
            dst_ref=dst,
            send_sem=sem_out,
            recv_sem=sem_in,
            device_id=device,
            device_id_type=MESH,
        ).start()

    def taken(ref, sem):
        pltpu.make_async_copy(ref, ref, sem).wait()

    def chunk_of(ref, chunk):
        return ref.at[pl.ds(0, DOM - 1), :, pl.ds(STARTS[chunk], WIDTHS[chunk])]

    def send_chunk(chunk):
        def body(i, carry):
            peer = dom_peer(i, dom)
            start = pl.multiple_of(peer * SLAB + STARTS[chunk], 128)
            send_to(
                particles.at[:, pl.ds(start, WIDTHS[chunk])],
                x_ref.at[dom, :, pl.ds(STARTS[chunk], WIDTHS[chunk])],
                send.at[2],
                x_recv.at[chunk],
                (cls, peer),
            )
            return carry

        lax.fori_loop(0, DOM - 1, body, 0)

    def send_codes(i, carry):
        send_to(codes, c_ref.at[dom], send.at[0], misc_recv.at[0], (cls, dom_peer(i, dom)))
        return carry

    def send_panels(i, carry):
        send_to(
            references.at[:, pl.ds(slab_start, SLAB)],
            r_ref.at[cls],
            send.at[1],
            misc_recv.at[1],
            ((cls + i) % CLS, dom),
        )
        return carry

    send_chunk(0)
    lax.fori_loop(0, DOM - 1, send_codes, 0)
    lax.fori_loop(1, CLS, send_panels, 0)
    for chunk in range(1, CHUNKS):
        send_chunk(chunk)

    taken(c_ref.at[pl.ds(0, DOM - 1)], misc_recv.at[0])
    code = jnp.sum(c_ref[...].reshape(8, 4, 128), axis=1)
    code_row = jnp.concatenate([code[t : t + 1] for t in range(8)], axis=1)
    group_row = code_row // BINS
    orient_row = code_row % BINS
    members = jnp.broadcast_to(group_row, (GROUPS, MEMBERS))
    hot_f32 = (lax.broadcasted_iota(jnp.int32, (GROUPS, MEMBERS), 0) == members).astype(F32)
    hot_t[...] = hot_f32.astype(BF16)
    counts = jnp.sum(hot_f32, axis=1, keepdims=True)
    group_col = jnp.transpose(jnp.broadcast_to(group_row.astype(F32), (128, MEMBERS)))
    lanes = lax.broadcasted_iota(jnp.int32, (MEMBERS, 128), 1).astype(F32)
    for half in range(GROUPS // 128):
        hot[:, 128 * half : 128 * half + 128] = (
            (group_col == lanes + float(128 * half)).astype(F32).astype(BF16)
        )
    score_sum[...] = jnp.zeros_like(score_sum)
    energy_sum[...] = jnp.zeros_like(energy_sum)

    taken(r_ref.at[pl.ds(0, CLS - 1)], misc_recv.at[1])
    for copy in own_copies:
        copy.wait()

    def whiten(part, carry):
        for chunk in range(CHUNKS):

            @pl.when(part == STARTS[chunk] // WIDE)
            def _():
                taken(chunk_of(x_ref, chunk), x_recv.at[chunk])

        lanes = pl.ds(pl.multiple_of(part * WIDE, WIDE), WIDE)
        values = x_ref[:, :, lanes].reshape(MEMBERS, WIDE).astype(F32)
        power = dot(hot_t[...], jnp.concatenate(split(values * values, 2), axis=1))
        inverse = (counts + 1.0) / (power[:, :WIDE] + power[:, WIDE:] + 1.0)
        parts = split(inverse, 3)
        spread = dot(hot[...], jnp.concatenate(parts[:2], axis=1))
        whitened = (values * (spread[:, :WIDE] + spread[:, WIDE:])).astype(BF16)
        x_ref[:, :, lanes] = whitened.reshape(DOM, ROWS, WIDE)
        panels = r_ref[:, :, lanes].reshape(PANELS, WIDE)
        score_sum[...] += dot_nt(panels, whitened)
        wide = panels.astype(F32)
        high, low = split(wide * wide, 2)
        squares = jnp.concatenate([high, high, high, low, low, low], axis=1)
        energy_sum[...] += dot_nt(squares, jnp.concatenate(parts + parts, axis=1))
        return carry

    lax.fori_loop(0, SLAB // WIDE, whiten, 0)

    spread_energy = jnp.zeros((PANELS, MEMBERS), F32)
    for part in split(energy_sum[...], 3):
        spread_energy += dot(part, hot_t[...])
    combined = (score_sum[...] - 0.5 * spread_energy).reshape(CLASSES, BINS, MEMBERS)
    bin_index = lax.broadcasted_iota(jnp.int32, (BINS, MEMBERS), 0)
    in_bin = bin_index == jnp.broadcast_to(orient_row, (BINS, MEMBERS))
    partial = jnp.sum(jnp.where(in_bin[None], combined, 0.0), axis=1)
    for q in range(4):
        for t in range(8):
            piece_out[q * 8 + t] = partial[4 * q : 4 * q + 4, 128 * t : 128 * t + 128]

    def send_piece(i, carry):
        peer = dom_peer(i, dom)
        send_to(piece_out.at[peer], piece_in.at[dom], send.at[3], misc_recv.at[2], (cls, peer))
        return carry

    lax.fori_loop(0, DOM - 1, send_piece, 0)
    piece_in[dom] = piece_out[dom]
    taken(piece_in.at[pl.ds(0, DOM - 1)], misc_recv.at[2])
    piece_all[dom] = jnp.sum(piece_in[...], axis=0)

    def send_sum(i, carry):
        peer = dom_peer(i, dom)
        send_to(piece_all.at[dom], piece_all.at[dom], send.at[4], misc_recv.at[3], (cls, peer))
        return carry

    lax.fori_loop(0, DOM - 1, send_sum, 0)
    taken(piece_all.at[pl.ds(0, DOM - 1)], misc_recv.at[3])
    for q in range(4):
        for t in range(8):
            scores_ref[4 * q : 4 * q + 4, 128 * t : 128 * t + 128] = piece_all[q * 8 + t]

    scores = scores_ref[...] * (1.0 / math.sqrt(DOM * SLAB))
    power = jnp.exp(scores - jnp.max(scores, axis=0, keepdims=True))
    weights = (power / jnp.sum(power, axis=0, keepdims=True)).astype(BF16).astype(F32)
    coefficient_f32 = jnp.where(in_bin[None], weights[:, None, :], 0.0).reshape(PANELS, MEMBERS)
    coefficient_ref[...] = coefficient_f32.astype(BF16)
    totals = jnp.sum(coefficient_f32, axis=1, keepdims=True)
    lane = lax.broadcasted_iota(jnp.int32, (PANELS, 128), 1)
    tail = jnp.zeros((PANELS, 128), F32)
    for k, piece in enumerate(split(totals, 3)):
        tail = jnp.where(lane == k, piece.astype(F32), tail)
    acc_out[:, :, SLAB:] = tail.astype(BF16).reshape(CLS, OWN, 128)
    for half in range(4):
        lanes = slice(half * 256, half * 256 + 256)
        acc_out[:, :, lanes] = (
            dot(coefficient_ref[...], x_ref[:, :, lanes].reshape(MEMBERS, 256))
            .astype(BF16)
            .reshape(CLS, OWN, 256)
        )

    def send_acc(i, carry):
        peer = (cls + i) % CLS
        send_to(acc_out.at[peer], acc_in.at[cls], send.at[5], misc_recv.at[4], (peer, dom))
        return carry

    lax.fori_loop(1, CLS, send_acc, 0)
    acc_in[cls] = acc_out[cls]
    taken(acc_in.at[pl.ds(0, CLS - 1)], misc_recv.at[4])
    total = jnp.sum(
        jnp.sum(acc_in[:, :, SLAB:].astype(F32), axis=0), axis=1, keepdims=True
    )
    out[...] = jnp.sum(acc_in[:, :, :SLAB].astype(F32), axis=0) / (total + 1.0)

    taken(c_ref.at[pl.ds(0, DOM - 1)], send.at[0])
    taken(r_ref.at[pl.ds(0, CLS - 1)], send.at[1])
    taken(x_ref.at[pl.ds(0, DOM - 1)], send.at[2])
    taken(piece_in.at[pl.ds(0, DOM - 1)], send.at[3])
    taken(piece_all.at[pl.ds(0, DOM - 1)], send.at[4])
    taken(acc_in.at[pl.ds(0, CLS - 1)], send.at[5])


def shards(particles, references, orient_bins, destinations, group_slots):
    hbm = pl.BlockSpec(memory_space=pltpu.HBM)
    out = pl.pallas_call(
        kernel,
        out_shape=jax.ShapeDtypeStruct((OWN, SLAB), F32),
        in_specs=[hbm] * 5,
        out_specs=pl.BlockSpec(memory_space=pltpu.VMEM),
        scratch_shapes=[
            pltpu.VMEM((DOM, ROWS, SLAB), BF16),
            pltpu.VMEM((3, 1, ROWS), jnp.int32),
            pltpu.VMEM((1, 128), jnp.int32),
            pltpu.VMEM((CLS, OWN, SLAB), BF16),
            pltpu.VMEM((DOM, 1, 128), jnp.int32),
            pltpu.VMEM((GROUPS, MEMBERS), BF16),
            pltpu.VMEM((MEMBERS, GROUPS), BF16),
            pltpu.VMEM((PANELS, MEMBERS), F32),
            pltpu.VMEM((PANELS, GROUPS), F32),
            pltpu.VMEM((DOM, 4, 128), F32),
            pltpu.VMEM((DOM, 4, 128), F32),
            pltpu.VMEM((DOM, 4, 128), F32),
            pltpu.VMEM((CLASSES, MEMBERS), F32),
            pltpu.VMEM((PANELS, MEMBERS), BF16),
            pltpu.VMEM((CLS, OWN, SLAB + 128), BF16),
            pltpu.VMEM((CLS, OWN, SLAB + 128), BF16),
            pltpu.SemaphoreType.DMA((CHUNKS,)),
            pltpu.SemaphoreType.DMA((5,)),
            pltpu.SemaphoreType.DMA((6,)),
            pltpu.SemaphoreType.DMA((5,)),
        ],
        compiler_params=pltpu.CompilerParams(
            collective_id=0, has_side_effects=True, vmem_limit_bytes=48 * 1024 * 1024
        ),
    )(
        *(
            pltpu.with_memory_space_constraint(value, pltpu.HBM)
            for value in (
                particles,
                references.reshape(OWN, DOM * SLAB),
                orient_bins.reshape(1, ROWS),
                destinations.reshape(1, ROWS),
                group_slots.reshape(1, ROWS),
            )
        )
    )
    return out.reshape(CLASSES // CLS, BINS, SLAB)


def solution(mesh):
    in_specs = (
        P(("cls", "dom"), None),
        P("cls", None, None),
        P(("cls", "dom")),
        P(("cls", "dom"), None),
        P(("cls", "dom")),
    )
    out_specs = P("cls", None, "dom")
    return jax.shard_map(shards, mesh=mesh, in_specs=in_specs, out_specs=out_specs, check_vma=False)
```

```python
import functools
import math

import jax
import jax.numpy as jnp
from jax import lax
from jax.experimental import pallas as pl
from jax.experimental.pallas import tpu as pltpu
from jax.sharding import PartitionSpec as P

MESH = pl.DeviceIdType.MESH
F32 = jnp.float32
BF16 = jnp.bfloat16

ROWS = 32
DOM = 32
CLS = 8
BINS = 8
CLASSES = 16
GROUPS = 256
MEMBERS = ROWS * DOM
SLAB = 1024
WIDTHS = (256, 256, 256, 128, 128)
STARTS = tuple(sum(WIDTHS[:c]) for c in range(len(WIDTHS)))
CHUNKS = len(WIDTHS)
WIDE = 128
PANELS = CLASSES * BINS
OWN = PANELS // CLS
Z = 8
Y = 4
STEPS = ((1, 2), (1, 1), (1, 3), (1, 0), (0, 2), (0, 1), (0, 3))

NT = (((1,), (1,)), ((), ()))


def dot(a, b):
    return jnp.dot(a, b, preferred_element_type=F32)


def dot_nt(a, b):
    return lax.dot_general(a, b, NT, preferred_element_type=F32)


def split(value, pieces):
    out = []
    for _ in range(pieces):
        piece = value.astype(BF16)
        out.append(piece)
        value = value - piece.astype(F32)
    return out


def dom_peer(i, dom):
    core, z, x = dom % 2, (dom // 2) % Z, dom // (2 * Z)
    j = i // 4
    step = 4 + (1 - 2 * (j % 2)) * ((j + 1) // 2)
    core = (core + 1 - i % 2) % 2
    x = (x + 1 - (i // 2) % 2) % 2
    z = (z + step) % Z
    return (x * Z + z) * 2 + core


def kernel(
    particles,
    references,
    orient_bins,
    destinations,
    group_slots,
    out,
    *scratch,
):
    (
        x_ref,
        rows,
        labels,
        codes,
        r_ref,
        c_ref,
        hot_t,
        hot,
        score_sum,
        energy_sum,
        piece_out,
        piece_in,
        piece_all,
        scores_ref,
        coefficient_ref,
        tot_out,
        tot_in,
        tot_col,
        acc_out,
        acc_in,
        x_recv,
        misc_recv,
        send,
        local,
    ) = scratch
    cls = lax.axis_index("cls")
    dom = lax.axis_index("dom")

    barrier = pltpu.get_barrier_semaphore()

    def greet_dom(i, carry):
        pl.semaphore_signal(barrier, inc=1, device_id=(cls, dom_peer(i, dom)), device_id_type=MESH)
        return carry

    def greet_cls(i, carry):
        pl.semaphore_signal(barrier, inc=1, device_id=((cls + i) % CLS, dom), device_id_type=MESH)
        return carry

    lax.fori_loop(0, DOM - 1, greet_dom, 0)
    lax.fori_loop(1, CLS, greet_cls, 0)

    slab_start = pl.multiple_of(dom * SLAB, SLAB)

    label_copies = [
        pltpu.make_async_copy(ref, labels.at[k], local.at[k])
        for k, ref in enumerate((destinations, group_slots, orient_bins))
    ]
    own_copies = [
        pltpu.make_async_copy(references.at[:, pl.ds(slab_start, SLAB)], r_ref.at[cls], local.at[3])
    ]
    staged = pltpu.make_async_copy(particles, rows, local.at[4])
    for copy in label_copies + own_copies + [staged]:
        copy.start()

    for copy in label_copies:
        copy.wait()
    own_code = (labels[0] * 8 + labels[1]) * BINS + labels[2]
    lane = lax.broadcasted_iota(jnp.int32, (1, 128), 1)
    four = jnp.concatenate([own_code] * 4, axis=1)
    codes[...] = jnp.where(lane // ROWS == dom % 4, four, 0)
    c_ref[dom] = codes[...]

    staged.wait()
    x_ref[dom] = rows[:, pl.ds(slab_start, SLAB)]
    pl.semaphore_wait(barrier, DOM - 1 + CLS - 1)

    def send_to(src, dst, sem_out, sem_in, device):
        pltpu.make_async_remote_copy(
            src_ref=src,
            dst_ref=dst,
            send_sem=sem_out,
            recv_sem=sem_in,
            device_id=device,
            device_id_type=MESH,
        ).start()

    def taken(ref, sem):
        pltpu.make_async_copy(ref, ref, sem).wait()

    def chunk_of(ref, chunk):
        return ref.at[pl.ds(0, DOM - 1), :, pl.ds(STARTS[chunk], WIDTHS[chunk])]

    def send_chunk(chunk):
        def body(i, carry):
            peer = dom_peer(i, dom)
            start = pl.multiple_of(peer * SLAB + STARTS[chunk], 128)
            send_to(
                rows.at[:, pl.ds(start, WIDTHS[chunk])],
                x_ref.at[dom, :, pl.ds(STARTS[chunk], WIDTHS[chunk])],
                send.at[2],
                x_recv.at[chunk],
                (cls, peer),
            )
            return carry

        lax.fori_loop(0, DOM - 1, body, 0)

    def send_codes(i, carry):
        send_to(codes, c_ref.at[dom], send.at[0], misc_recv.at[0], (cls, dom_peer(i, dom)))
        return carry

    def send_panels(i, carry):
        send_to(
            references.at[:, pl.ds(slab_start, SLAB)],
            r_ref.at[cls],
            send.at[1],
            misc_recv.at[1],
            ((cls + i) % CLS, dom),
        )
        return carry

    send_chunk(0)
    lax.fori_loop(0, DOM - 1, send_codes, 0)
    lax.fori_loop(1, CLS, send_panels, 0)
    for chunk in range(1, CHUNKS):
        send_chunk(chunk)

    taken(c_ref.at[pl.ds(0, DOM - 1)], misc_recv.at[0])
    code = jnp.sum(c_ref[...].reshape(8, 4, 128), axis=1)
    code_row = jnp.concatenate([code[t : t + 1] for t in range(8)], axis=1)
    group_row = code_row // BINS
    orient_row = code_row % BINS
    members = jnp.broadcast_to(group_row, (GROUPS, MEMBERS))
    hot_f32 = (lax.broadcasted_iota(jnp.int32, (GROUPS, MEMBERS), 0) == members).astype(F32)
    hot_t[...] = hot_f32.astype(BF16)
    counts = jnp.sum(hot_f32, axis=1, keepdims=True)
    group_col = jnp.transpose(jnp.broadcast_to(group_row.astype(F32), (128, MEMBERS)))
    lanes = lax.broadcasted_iota(jnp.int32, (MEMBERS, 128), 1).astype(F32)
    for half in range(GROUPS // 128):
        hot[:, 128 * half : 128 * half + 128] = (
            (group_col == lanes + float(128 * half)).astype(F32).astype(BF16)
        )
    score_sum[...] = jnp.zeros_like(score_sum)
    energy_sum[...] = jnp.zeros_like(energy_sum)

    taken(r_ref.at[pl.ds(0, CLS - 1)], misc_recv.at[1])
    for copy in own_copies:
        copy.wait()

    def whiten(part, carry):
        for chunk in range(CHUNKS):

            @pl.when(part == STARTS[chunk] // WIDE)
            def _():
                taken(chunk_of(x_ref, chunk), x_recv.at[chunk])

        lanes = pl.ds(pl.multiple_of(part * WIDE, WIDE), WIDE)
        values = x_ref[:, :, lanes].reshape(MEMBERS, WIDE).astype(F32)
        power = dot(hot_t[...], jnp.concatenate(split(values * values, 2), axis=1))
        inverse = (counts + 1.0) / (power[:, :WIDE] + power[:, WIDE:] + 1.0)
        parts = split(inverse, 3)
        spread = dot(hot[...], jnp.concatenate(parts[:2], axis=1))
        whitened = (values * (spread[:, :WIDE] + spread[:, WIDE:])).astype(BF16)
        x_ref[:, :, lanes] = whitened.reshape(DOM, ROWS, WIDE)
        panels = r_ref[:, :, lanes].reshape(PANELS, WIDE)
        score_sum[...] += dot_nt(panels, whitened)
        wide = panels.astype(F32)
        high, low = split(wide * wide, 2)
        squares = jnp.concatenate([high, high, high, low, low, low], axis=1)
        energy_sum[...] += dot_nt(squares, jnp.concatenate(parts + parts, axis=1))
        return carry

    lax.fori_loop(0, SLAB // WIDE, whiten, 0)

    spread_energy = jnp.zeros((PANELS, MEMBERS), F32)
    for part in split(energy_sum[...], 3):
        spread_energy += dot(part, hot_t[...])
    combined = (score_sum[...] - 0.5 * spread_energy).reshape(CLASSES, BINS, MEMBERS)
    bin_index = lax.broadcasted_iota(jnp.int32, (BINS, MEMBERS), 0)
    in_bin = bin_index == jnp.broadcast_to(orient_row, (BINS, MEMBERS))
    partial = jnp.sum(jnp.where(in_bin[None], combined, 0.0), axis=1)
    for q in range(4):
        for t in range(8):
            piece_out[q * 8 + t] = partial[4 * q : 4 * q + 4, 128 * t : 128 * t + 128]

    def send_piece(i, carry):
        peer = dom_peer(i, dom)
        send_to(piece_out.at[peer], piece_in.at[dom], send.at[3], misc_recv.at[2], (cls, peer))
        return carry

    lax.fori_loop(0, DOM - 1, send_piece, 0)
    piece_in[dom] = piece_out[dom]
    taken(piece_in.at[pl.ds(0, DOM - 1)], misc_recv.at[2])
    piece_all[dom] = jnp.sum(piece_in[...], axis=0)

    def send_sum(i, carry):
        peer = dom_peer(i, dom)
        send_to(piece_all.at[dom], piece_all.at[dom], send.at[4], misc_recv.at[3], (cls, peer))
        return carry

    lax.fori_loop(0, DOM - 1, send_sum, 0)
    taken(piece_all.at[pl.ds(0, DOM - 1)], misc_recv.at[3])
    for q in range(4):
        for t in range(8):
            scores_ref[4 * q : 4 * q + 4, 128 * t : 128 * t + 128] = piece_all[q * 8 + t]

    scores = scores_ref[...] * (1.0 / math.sqrt(DOM * SLAB))
    power = jnp.exp(scores - jnp.max(scores, axis=0, keepdims=True))
    weights = (power / jnp.sum(power, axis=0, keepdims=True)).astype(BF16).astype(F32)
    coefficient_f32 = jnp.where(in_bin[None], weights[:, None, :], 0.0).reshape(PANELS, MEMBERS)
    coefficient_ref[...] = coefficient_f32.astype(BF16)
    tot_out[...] = dot_nt(jnp.ones((16, MEMBERS), BF16), coefficient_ref[...])[0:1]

    peers = [((cls // Y + dx) % 2) * Y + (cls + dy) % Y for dx, dy in STEPS]
    for peer in peers:
        send_to(tot_out, tot_in.at[cls], send.at[6], misc_recv.at[5], (peer, dom))
    tot_in[cls] = tot_out[...]
    for start in range(0, SLAB, 256):
        acc_out[:, :, start : start + 256] = (
            dot(coefficient_ref[...], x_ref[:, :, start : start + 256].reshape(MEMBERS, 256))
            .astype(BF16)
            .reshape(CLS, OWN, 256)
        )
    for peer in peers:
        send_to(acc_out.at[peer], acc_in.at[cls], send.at[5], misc_recv.at[4], (peer, dom))
    acc_in[cls] = acc_out[cls]

    taken(tot_in.at[pl.ds(0, CLS - 1)], misc_recv.at[5])
    total = jnp.sum(tot_in[...], axis=0)
    tot_col[...] = jnp.transpose(jnp.broadcast_to(total, (PANELS, 128)))
    own_total = tot_col[pl.ds(pl.multiple_of(cls * OWN, OWN), OWN), 0:1]
    taken(acc_in.at[pl.ds(0, CLS - 1)], misc_recv.at[4])
    out[...] = jnp.sum(acc_in[...].astype(F32), axis=0) / (own_total + 1.0)

    taken(c_ref.at[pl.ds(0, DOM - 1)], send.at[0])
    taken(r_ref.at[pl.ds(0, CLS - 1)], send.at[1])
    taken(x_ref.at[pl.ds(0, DOM - 1)], send.at[2])
    taken(piece_in.at[pl.ds(0, DOM - 1)], send.at[3])
    taken(piece_all.at[pl.ds(0, DOM - 1)], send.at[4])
    taken(acc_in.at[pl.ds(0, CLS - 1)], send.at[5])
    taken(tot_in.at[pl.ds(0, CLS - 1)], send.at[6])


def shards(particles, references, orient_bins, destinations, group_slots):
    hbm = pl.BlockSpec(memory_space=pltpu.HBM)
    out = pl.pallas_call(
        kernel,
        out_shape=jax.ShapeDtypeStruct((OWN, SLAB), F32),
        in_specs=[hbm] * 5,
        out_specs=pl.BlockSpec(memory_space=pltpu.VMEM),
        scratch_shapes=[
            pltpu.VMEM((DOM, ROWS, SLAB), BF16),
            pltpu.VMEM((ROWS, DOM * SLAB), BF16),
            pltpu.VMEM((3, 1, ROWS), jnp.int32),
            pltpu.VMEM((1, 128), jnp.int32),
            pltpu.VMEM((CLS, OWN, SLAB), BF16),
            pltpu.VMEM((DOM, 1, 128), jnp.int32),
            pltpu.VMEM((GROUPS, MEMBERS), BF16),
            pltpu.VMEM((MEMBERS, GROUPS), BF16),
            pltpu.VMEM((PANELS, MEMBERS), F32),
            pltpu.VMEM((PANELS, GROUPS), F32),
            pltpu.VMEM((DOM, 4, 128), F32),
            pltpu.VMEM((DOM, 4, 128), F32),
            pltpu.VMEM((DOM, 4, 128), F32),
            pltpu.VMEM((CLASSES, MEMBERS), F32),
            pltpu.VMEM((PANELS, MEMBERS), BF16),
            pltpu.VMEM((1, PANELS), F32),
            pltpu.VMEM((CLS, 1, PANELS), F32),
            pltpu.VMEM((PANELS, 128), F32),
            pltpu.VMEM((CLS, OWN, SLAB), BF16),
            pltpu.VMEM((CLS, OWN, SLAB), BF16),
            pltpu.SemaphoreType.DMA((CHUNKS,)),
            pltpu.SemaphoreType.DMA((6,)),
            pltpu.SemaphoreType.DMA((7,)),
            pltpu.SemaphoreType.DMA((5,)),
        ],
        compiler_params=pltpu.CompilerParams(
            collective_id=0, has_side_effects=True, vmem_limit_bytes=48 * 1024 * 1024
        ),
    )(
        *(
            pltpu.with_memory_space_constraint(value, pltpu.HBM)
            for value in (
                particles,
                references.reshape(OWN, DOM * SLAB),
                orient_bins.reshape(1, ROWS),
                destinations.reshape(1, ROWS),
                group_slots.reshape(1, ROWS),
            )
        )
    )
    return out.reshape(CLASSES // CLS, BINS, SLAB)


def solution(mesh):
    in_specs = (
        P(("cls", "dom"), None),
        P("cls", None, None),
        P(("cls", "dom")),
        P(("cls", "dom"), None),
        P(("cls", "dom")),
    )
    out_specs = P("cls", None, "dom")
    return jax.shard_map(shards, mesh=mesh, in_specs=in_specs, out_specs=out_specs, check_vma=False)
```

```python
import functools
import math

import jax
import jax.numpy as jnp
from jax import lax
from jax.experimental import pallas as pl
from jax.experimental.pallas import tpu as pltpu
from jax.sharding import PartitionSpec as P

MESH = pl.DeviceIdType.MESH
F32 = jnp.float32
BF16 = jnp.bfloat16

ROWS = 32
DOM = 32
CLS = 8
BINS = 8
CLASSES = 16
GROUPS = 256
MEMBERS = ROWS * DOM
SLAB = 1024
WIDTHS = (512, 384, 128)
STARTS = tuple(sum(WIDTHS[:c]) for c in range(len(WIDTHS)))
CHUNKS = len(WIDTHS)
WIDE = 128
PANELS = CLASSES * BINS
OWN = PANELS // CLS
Z = 8
Y = 4
STEPS = ((1, 2), (1, 1), (1, 3), (1, 0), (0, 2), (0, 1), (0, 3))

NT = (((1,), (1,)), ((), ()))


def dot(a, b):
    return jnp.dot(a, b, preferred_element_type=F32)


def dot_nt(a, b):
    return lax.dot_general(a, b, NT, preferred_element_type=F32)


def split(value, pieces):
    out = []
    for _ in range(pieces):
        piece = value.astype(BF16)
        out.append(piece)
        value = value - piece.astype(F32)
    return out


def dom_peer(i, dom):
    core, z, x = dom % 2, (dom // 2) % Z, dom // (2 * Z)
    j = i // 4
    step = 4 + (1 - 2 * (j % 2)) * ((j + 1) // 2)
    core = (core + 1 - i % 2) % 2
    x = (x + 1 - (i // 2) % 2) % 2
    z = (z + step) % Z
    return (x * Z + z) * 2 + core


def kernel(
    particles,
    references,
    orient_bins,
    destinations,
    group_slots,
    out,
    *scratch,
):
    (
        x_ref,
        rows,
        labels,
        codes,
        r_ref,
        c_ref,
        hot_t,
        hot,
        score_sum,
        energy_sum,
        piece_out,
        piece_in,
        piece_all,
        scores_ref,
        coefficient_ref,
        tot_out,
        tot_in,
        tot_col,
        acc_out,
        acc_in,
        x_recv,
        misc_recv,
        send,
        local,
    ) = scratch
    cls = lax.axis_index("cls")
    dom = lax.axis_index("dom")

    barrier = pltpu.get_barrier_semaphore()

    def greet_dom(i, carry):
        pl.semaphore_signal(barrier, inc=1, device_id=(cls, dom_peer(i, dom)), device_id_type=MESH)
        return carry

    def greet_cls(i, carry):
        pl.semaphore_signal(barrier, inc=1, device_id=((cls + i) % CLS, dom), device_id_type=MESH)
        return carry

    lax.fori_loop(0, DOM - 1, greet_dom, 0)
    lax.fori_loop(1, CLS, greet_cls, 0)

    slab_start = pl.multiple_of(dom * SLAB, SLAB)

    label_copies = [
        pltpu.make_async_copy(ref, labels.at[k], local.at[k])
        for k, ref in enumerate((destinations, group_slots, orient_bins))
    ]
    own_copies = [
        pltpu.make_async_copy(references.at[:, pl.ds(slab_start, SLAB)], r_ref.at[cls], local.at[3])
    ]
    staged = pltpu.make_async_copy(particles, rows, local.at[4])
    for copy in label_copies + own_copies + [staged]:
        copy.start()

    for copy in label_copies:
        copy.wait()
    own_code = (labels[0] * 8 + labels[1]) * BINS + labels[2]
    lane = lax.broadcasted_iota(jnp.int32, (1, 128), 1)
    four = jnp.concatenate([own_code] * 4, axis=1)
    codes[...] = jnp.where(lane // ROWS == dom % 4, four, 0)
    c_ref[dom] = codes[...]

    staged.wait()
    x_ref[dom] = rows[:, pl.ds(slab_start, SLAB)]
    pl.semaphore_wait(barrier, DOM - 1 + CLS - 1)

    def send_to(src, dst, sem_out, sem_in, device):
        pltpu.make_async_remote_copy(
            src_ref=src,
            dst_ref=dst,
            send_sem=sem_out,
            recv_sem=sem_in,
            device_id=device,
            device_id_type=MESH,
        ).start()

    def taken(ref, sem):
        pltpu.make_async_copy(ref, ref, sem).wait()

    def chunk_of(ref, chunk):
        return ref.at[pl.ds(0, DOM - 1), :, pl.ds(STARTS[chunk], WIDTHS[chunk])]

    def send_chunk(chunk):
        def body(i, carry):
            peer = dom_peer(i, dom)
            start = pl.multiple_of(peer * SLAB + STARTS[chunk], 128)
            send_to(
                rows.at[:, pl.ds(start, WIDTHS[chunk])],
                x_ref.at[dom, :, pl.ds(STARTS[chunk], WIDTHS[chunk])],
                send.at[2],
                x_recv.at[chunk],
                (cls, peer),
            )
            return carry

        lax.fori_loop(0, DOM - 1, body, 0)

    def send_codes(i, carry):
        send_to(codes, c_ref.at[dom], send.at[0], misc_recv.at[0], (cls, dom_peer(i, dom)))
        return carry

    def send_panels(i, carry):
        send_to(
            references.at[:, pl.ds(slab_start, SLAB)],
            r_ref.at[cls],
            send.at[1],
            misc_recv.at[1],
            ((cls + i) % CLS, dom),
        )
        return carry

    send_chunk(0)
    lax.fori_loop(0, DOM - 1, send_codes, 0)
    lax.fori_loop(1, CLS, send_panels, 0)
    for chunk in range(1, CHUNKS):
        send_chunk(chunk)

    taken(c_ref.at[pl.ds(0, DOM - 1)], misc_recv.at[0])
    code = jnp.sum(c_ref[...].reshape(8, 4, 128), axis=1)
    code_row = jnp.concatenate([code[t : t + 1] for t in range(8)], axis=1)
    group_row = code_row // BINS
    orient_row = code_row % BINS
    members = jnp.broadcast_to(group_row, (GROUPS, MEMBERS))
    hot_f32 = (lax.broadcasted_iota(jnp.int32, (GROUPS, MEMBERS), 0) == members).astype(F32)
    hot_t[...] = hot_f32.astype(BF16)
    counts = jnp.sum(hot_f32, axis=1, keepdims=True)
    group_col = jnp.transpose(jnp.broadcast_to(group_row.astype(F32), (128, MEMBERS)))
    lanes = lax.broadcasted_iota(jnp.int32, (MEMBERS, 128), 1).astype(F32)
    for half in range(GROUPS // 128):
        hot[:, 128 * half : 128 * half + 128] = (
            (group_col == lanes + float(128 * half)).astype(F32).astype(BF16)
        )
    score_sum[...] = jnp.zeros_like(score_sum)
    energy_sum[...] = jnp.zeros_like(energy_sum)

    taken(r_ref.at[pl.ds(0, CLS - 1)], misc_recv.at[1])
    for copy in own_copies:
        copy.wait()

    def whiten(part, carry):
        for chunk in range(CHUNKS):

            @pl.when(part == STARTS[chunk] // WIDE)
            def _():
                taken(chunk_of(x_ref, chunk), x_recv.at[chunk])

        lanes = pl.ds(pl.multiple_of(part * WIDE, WIDE), WIDE)
        values = x_ref[:, :, lanes].reshape(MEMBERS, WIDE).astype(F32)
        power = dot(hot_t[...], jnp.concatenate(split(values * values, 2), axis=1))
        inverse = (counts + 1.0) / (power[:, :WIDE] + power[:, WIDE:] + 1.0)
        parts = split(inverse, 3)
        spread = dot(hot[...], jnp.concatenate(parts[:2], axis=1))
        whitened = (values * (spread[:, :WIDE] + spread[:, WIDE:])).astype(BF16)
        x_ref[:, :, lanes] = whitened.reshape(DOM, ROWS, WIDE)
        panels = r_ref[:, :, lanes].reshape(PANELS, WIDE)
        score_sum[...] += dot_nt(panels, whitened)
        wide = panels.astype(F32)
        high, low = split(wide * wide, 2)
        squares = jnp.concatenate([high, high, high, low, low, low], axis=1)
        energy_sum[...] += dot_nt(squares, jnp.concatenate(parts + parts, axis=1))
        return carry

    lax.fori_loop(0, SLAB // WIDE, whiten, 0)

    spread_energy = jnp.zeros((PANELS, MEMBERS), F32)
    for part in split(energy_sum[...], 3):
        spread_energy += dot(part, hot_t[...])
    combined = (score_sum[...] - 0.5 * spread_energy).reshape(CLASSES, BINS, MEMBERS)
    bin_index = lax.broadcasted_iota(jnp.int32, (BINS, MEMBERS), 0)
    in_bin = bin_index == jnp.broadcast_to(orient_row, (BINS, MEMBERS))
    partial = jnp.sum(jnp.where(in_bin[None], combined, 0.0), axis=1)
    for q in range(4):
        for t in range(8):
            piece_out[q * 8 + t] = partial[4 * q : 4 * q + 4, 128 * t : 128 * t + 128]

    def send_piece(i, carry):
        peer = dom_peer(i, dom)
        send_to(piece_out.at[peer], piece_in.at[dom], send.at[3], misc_recv.at[2], (cls, peer))
        return carry

    lax.fori_loop(0, DOM - 1, send_piece, 0)
    piece_in[dom] = piece_out[dom]
    taken(piece_in.at[pl.ds(0, DOM - 1)], misc_recv.at[2])
    piece_all[dom] = jnp.sum(piece_in[...], axis=0)

    def send_sum(i, carry):
        peer = dom_peer(i, dom)
        send_to(piece_all.at[dom], piece_all.at[dom], send.at[4], misc_recv.at[3], (cls, peer))
        return carry

    lax.fori_loop(0, DOM - 1, send_sum, 0)
    taken(piece_all.at[pl.ds(0, DOM - 1)], misc_recv.at[3])
    for q in range(4):
        for t in range(8):
            scores_ref[4 * q : 4 * q + 4, 128 * t : 128 * t + 128] = piece_all[q * 8 + t]

    scores = scores_ref[...] * (1.0 / math.sqrt(DOM * SLAB))
    power = jnp.exp(scores - jnp.max(scores, axis=0, keepdims=True))
    weights = (power / jnp.sum(power, axis=0, keepdims=True)).astype(BF16).astype(F32)
    coefficient_f32 = jnp.where(in_bin[None], weights[:, None, :], 0.0).reshape(PANELS, MEMBERS)
    coefficient_ref[...] = coefficient_f32.astype(BF16)
    tot_out[...] = dot_nt(jnp.ones((16, MEMBERS), BF16), coefficient_ref[...])[0:1]

    peers = [((cls // Y + dx) % 2) * Y + (cls + dy) % Y for dx, dy in STEPS]
    for peer in peers:
        send_to(tot_out, tot_in.at[cls], send.at[6], misc_recv.at[5], (peer, dom))
    tot_in[cls] = tot_out[...]
    for start in range(0, SLAB, 256):
        acc_out[:, :, start : start + 256] = (
            dot(coefficient_ref[...], x_ref[:, :, start : start + 256].reshape(MEMBERS, 256))
            .astype(BF16)
            .reshape(CLS, OWN, 256)
        )
    for peer in peers:
        send_to(acc_out.at[peer], acc_in.at[cls], send.at[5], misc_recv.at[4], (peer, dom))
    acc_in[cls] = acc_out[cls]

    taken(tot_in.at[pl.ds(0, CLS - 1)], misc_recv.at[5])
    total = jnp.sum(tot_in[...], axis=0)
    tot_col[...] = jnp.transpose(jnp.broadcast_to(total, (PANELS, 128)))
    own_total = tot_col[pl.ds(pl.multiple_of(cls * OWN, OWN), OWN), 0:1]
    taken(acc_in.at[pl.ds(0, CLS - 1)], misc_recv.at[4])
    out[...] = jnp.sum(acc_in[...].astype(F32), axis=0) / (own_total + 1.0)

    taken(c_ref.at[pl.ds(0, DOM - 1)], send.at[0])
    taken(r_ref.at[pl.ds(0, CLS - 1)], send.at[1])
    taken(x_ref.at[pl.ds(0, DOM - 1)], send.at[2])
    taken(piece_in.at[pl.ds(0, DOM - 1)], send.at[3])
    taken(piece_all.at[pl.ds(0, DOM - 1)], send.at[4])
    taken(acc_in.at[pl.ds(0, CLS - 1)], send.at[5])
    taken(tot_in.at[pl.ds(0, CLS - 1)], send.at[6])


def shards(particles, references, orient_bins, destinations, group_slots):
    hbm = pl.BlockSpec(memory_space=pltpu.HBM)
    out = pl.pallas_call(
        kernel,
        out_shape=jax.ShapeDtypeStruct((OWN, SLAB), F32),
        in_specs=[hbm] * 5,
        out_specs=pl.BlockSpec(memory_space=pltpu.VMEM),
        scratch_shapes=[
            pltpu.VMEM((DOM, ROWS, SLAB), BF16),
            pltpu.VMEM((ROWS, DOM * SLAB), BF16),
            pltpu.VMEM((3, 1, ROWS), jnp.int32),
            pltpu.VMEM((1, 128), jnp.int32),
            pltpu.VMEM((CLS, OWN, SLAB), BF16),
            pltpu.VMEM((DOM, 1, 128), jnp.int32),
            pltpu.VMEM((GROUPS, MEMBERS), BF16),
            pltpu.VMEM((MEMBERS, GROUPS), BF16),
            pltpu.VMEM((PANELS, MEMBERS), F32),
            pltpu.VMEM((PANELS, GROUPS), F32),
            pltpu.VMEM((DOM, 4, 128), F32),
            pltpu.VMEM((DOM, 4, 128), F32),
            pltpu.VMEM((DOM, 4, 128), F32),
            pltpu.VMEM((CLASSES, MEMBERS), F32),
            pltpu.VMEM((PANELS, MEMBERS), BF16),
            pltpu.VMEM((1, PANELS), F32),
            pltpu.VMEM((CLS, 1, PANELS), F32),
            pltpu.VMEM((PANELS, 128), F32),
            pltpu.VMEM((CLS, OWN, SLAB), BF16),
            pltpu.VMEM((CLS, OWN, SLAB), BF16),
            pltpu.SemaphoreType.DMA((CHUNKS,)),
            pltpu.SemaphoreType.DMA((6,)),
            pltpu.SemaphoreType.DMA((7,)),
            pltpu.SemaphoreType.DMA((5,)),
        ],
        compiler_params=pltpu.CompilerParams(
            collective_id=0, has_side_effects=True, vmem_limit_bytes=48 * 1024 * 1024
        ),
    )(
        *(
            pltpu.with_memory_space_constraint(value, pltpu.HBM)
            for value in (
                particles,
                references.reshape(OWN, DOM * SLAB),
                orient_bins.reshape(1, ROWS),
                destinations.reshape(1, ROWS),
                group_slots.reshape(1, ROWS),
            )
        )
    )
    return out.reshape(CLASSES // CLS, BINS, SLAB)


def solution(mesh):
    in_specs = (
        P(("cls", "dom"), None),
        P("cls", None, None),
        P(("cls", "dom")),
        P(("cls", "dom"), None),
        P(("cls", "dom")),
    )
    out_specs = P("cls", None, "dom")
    return jax.shard_map(shards, mesh=mesh, in_specs=in_specs, out_specs=out_specs, check_vma=False)
```

```python
import functools
import math

import jax
import jax.numpy as jnp
from jax import lax
from jax.experimental import pallas as pl
from jax.experimental.pallas import tpu as pltpu
from jax.sharding import PartitionSpec as P

MESH = pl.DeviceIdType.MESH
F32 = jnp.float32
BF16 = jnp.bfloat16

ROWS = 32
DOM = 32
CLS = 8
BINS = 8
CLASSES = 16
GROUPS = 256
MEMBERS = ROWS * DOM
SLAB = 1024
WIDTHS = (512, 384, 128)
STARTS = tuple(sum(WIDTHS[:c]) for c in range(len(WIDTHS)))
CHUNKS = len(WIDTHS)
WIDE = 128
PANELS = CLASSES * BINS
OWN = PANELS // CLS
Z = 8
Y = 4
STEPS = ((1, 2), (1, 1), (1, 3), (1, 0), (0, 2), (0, 1), (0, 3))

NT = (((1,), (1,)), ((), ()))


def dot(a, b):
    return jnp.dot(a, b, preferred_element_type=F32)


def dot_nt(a, b):
    return lax.dot_general(a, b, NT, preferred_element_type=F32)


def split(value, pieces):
    out = []
    for _ in range(pieces):
        piece = value.astype(BF16)
        out.append(piece)
        value = value - piece.astype(F32)
    return out


def dom_peer(i, dom):
    core, z, x = dom % 2, (dom // 2) % Z, dom // (2 * Z)
    j = i // 4
    step = 4 + (1 - 2 * (j % 2)) * ((j + 1) // 2)
    core = (core + 1 - i % 2) % 2
    x = (x + 1 - (i // 2) % 2) % 2
    z = (z + step) % Z
    return (x * Z + z) * 2 + core


def kernel(
    particles,
    references,
    orient_bins,
    destinations,
    group_slots,
    out,
    *scratch,
):
    (
        x_ref,
        rows,
        labels,
        codes,
        r_ref,
        c_ref,
        hot_t,
        hot,
        score_sum,
        energy_sum,
        piece_out,
        piece_in,
        piece_all,
        scores_ref,
        coefficient_ref,
        tot_out,
        tot_in,
        tot_col,
        acc_out,
        acc_in,
        x_recv,
        misc_recv,
        send,
        local,
    ) = scratch
    cls = lax.axis_index("cls")
    dom = lax.axis_index("dom")

    barrier = pltpu.get_barrier_semaphore()

    def greet_dom(i, carry):
        pl.semaphore_signal(barrier, inc=1, device_id=(cls, dom_peer(i, dom)), device_id_type=MESH)
        return carry

    def greet_cls(i, carry):
        pl.semaphore_signal(barrier, inc=1, device_id=((cls + i) % CLS, dom), device_id_type=MESH)
        return carry

    for i in range(DOM - 1):
        greet_dom(i, 0)
    lax.fori_loop(1, CLS, greet_cls, 0)

    slab_start = pl.multiple_of(dom * SLAB, SLAB)

    label_copies = [
        pltpu.make_async_copy(ref, labels.at[k], local.at[k])
        for k, ref in enumerate((destinations, group_slots, orient_bins))
    ]
    own_copies = [
        pltpu.make_async_copy(references.at[:, pl.ds(slab_start, SLAB)], r_ref.at[cls], local.at[3])
    ]
    staged = pltpu.make_async_copy(particles, rows, local.at[4])
    for copy in label_copies + own_copies + [staged]:
        copy.start()

    for copy in label_copies:
        copy.wait()
    own_code = (labels[0] * 8 + labels[1]) * BINS + labels[2]
    lane = lax.broadcasted_iota(jnp.int32, (1, 128), 1)
    four = jnp.concatenate([own_code] * 4, axis=1)
    codes[...] = jnp.where(lane // ROWS == dom % 4, four, 0)
    c_ref[dom] = codes[...]

    staged.wait()
    x_ref[dom] = rows[:, pl.ds(slab_start, SLAB)]
    pl.semaphore_wait(barrier, DOM - 1 + CLS - 1)

    def send_to(src, dst, sem_out, sem_in, device):
        pltpu.make_async_remote_copy(
            src_ref=src,
            dst_ref=dst,
            send_sem=sem_out,
            recv_sem=sem_in,
            device_id=device,
            device_id_type=MESH,
        ).start()

    def taken(ref, sem):
        pltpu.make_async_copy(ref, ref, sem).wait()

    def chunk_of(ref, chunk):
        return ref.at[pl.ds(0, DOM - 1), :, pl.ds(STARTS[chunk], WIDTHS[chunk])]

    def send_chunk(chunk):
        def body(i, carry):
            peer = dom_peer(i, dom)
            start = pl.multiple_of(peer * SLAB + STARTS[chunk], 128)
            send_to(
                rows.at[:, pl.ds(start, WIDTHS[chunk])],
                x_ref.at[dom, :, pl.ds(STARTS[chunk], WIDTHS[chunk])],
                send.at[2],
                x_recv.at[chunk],
                (cls, peer),
            )
            return carry

        lax.fori_loop(0, DOM - 1, body, 0)

    def send_codes(i, carry):
        send_to(codes, c_ref.at[dom], send.at[0], misc_recv.at[0], (cls, dom_peer(i, dom)))
        return carry

    def send_panels(i, carry):
        send_to(
            references.at[:, pl.ds(slab_start, SLAB)],
            r_ref.at[cls],
            send.at[1],
            misc_recv.at[1],
            ((cls + i) % CLS, dom),
        )
        return carry

    send_chunk(0)
    lax.fori_loop(0, DOM - 1, send_codes, 0)
    lax.fori_loop(1, CLS, send_panels, 0)
    for chunk in range(1, CHUNKS):
        send_chunk(chunk)

    taken(c_ref.at[pl.ds(0, DOM - 1)], misc_recv.at[0])
    code = jnp.sum(c_ref[...].reshape(8, 4, 128), axis=1)
    code_row = jnp.concatenate([code[t : t + 1] for t in range(8)], axis=1)
    group_row = code_row // BINS
    orient_row = code_row % BINS
    members = jnp.broadcast_to(group_row, (GROUPS, MEMBERS))
    hot_f32 = (lax.broadcasted_iota(jnp.int32, (GROUPS, MEMBERS), 0) == members).astype(F32)
    hot_t[...] = hot_f32.astype(BF16)
    counts = jnp.sum(hot_f32, axis=1, keepdims=True)
    group_col = jnp.transpose(jnp.broadcast_to(group_row.astype(F32), (128, MEMBERS)))
    lanes = lax.broadcasted_iota(jnp.int32, (MEMBERS, 128), 1).astype(F32)
    for half in range(GROUPS // 128):
        hot[:, 128 * half : 128 * half + 128] = (
            (group_col == lanes + float(128 * half)).astype(F32).astype(BF16)
        )
    score_sum[...] = jnp.zeros_like(score_sum)
    energy_sum[...] = jnp.zeros_like(energy_sum)

    taken(r_ref.at[pl.ds(0, CLS - 1)], misc_recv.at[1])
    for copy in own_copies:
        copy.wait()

    def whiten(part, carry):
        for chunk in range(CHUNKS):

            @pl.when(part == STARTS[chunk] // WIDE)
            def _():
                taken(chunk_of(x_ref, chunk), x_recv.at[chunk])

        lanes = pl.ds(pl.multiple_of(part * WIDE, WIDE), WIDE)
        values = x_ref[:, :, lanes].reshape(MEMBERS, WIDE).astype(F32)
        power = dot(hot_t[...], jnp.concatenate(split(values * values, 2), axis=1))
        inverse = (counts + 1.0) / (power[:, :WIDE] + power[:, WIDE:] + 1.0)
        parts = split(inverse, 3)
        spread = dot(hot[...], jnp.concatenate(parts[:2], axis=1))
        whitened = (values * (spread[:, :WIDE] + spread[:, WIDE:])).astype(BF16)
        x_ref[:, :, lanes] = whitened.reshape(DOM, ROWS, WIDE)
        panels = r_ref[:, :, lanes].reshape(PANELS, WIDE)
        score_sum[...] += dot_nt(panels, whitened)
        wide = panels.astype(F32)
        high, low = split(wide * wide, 2)
        squares = jnp.concatenate([high, high, high, low, low, low], axis=1)
        energy_sum[...] += dot_nt(squares, jnp.concatenate(parts + parts, axis=1))
        return carry

    lax.fori_loop(0, SLAB // WIDE, whiten, 0)

    spread_energy = jnp.zeros((PANELS, MEMBERS), F32)
    for part in split(energy_sum[...], 3):
        spread_energy += dot(part, hot_t[...])
    combined = (score_sum[...] - 0.5 * spread_energy).reshape(CLASSES, BINS, MEMBERS)
    bin_index = lax.broadcasted_iota(jnp.int32, (BINS, MEMBERS), 0)
    in_bin = bin_index == jnp.broadcast_to(orient_row, (BINS, MEMBERS))
    partial = jnp.sum(jnp.where(in_bin[None], combined, 0.0), axis=1)
    for q in range(4):
        for t in range(8):
            piece_out[q * 8 + t] = partial[4 * q : 4 * q + 4, 128 * t : 128 * t + 128]

    def send_piece(i, carry):
        peer = dom_peer(i, dom)
        send_to(piece_out.at[peer], piece_in.at[dom], send.at[3], misc_recv.at[2], (cls, peer))
        return carry

    for i in range(DOM - 1):
        send_piece(i, 0)
    piece_in[dom] = piece_out[dom]
    taken(piece_in.at[pl.ds(0, DOM - 1)], misc_recv.at[2])
    piece_all[dom] = jnp.sum(piece_in[...], axis=0)

    def send_sum(i, carry):
        peer = dom_peer(i, dom)
        send_to(piece_all.at[dom], piece_all.at[dom], send.at[4], misc_recv.at[3], (cls, peer))
        return carry

    for i in range(DOM - 1):
        send_sum(i, 0)
    taken(piece_all.at[pl.ds(0, DOM - 1)], misc_recv.at[3])
    for q in range(4):
        for t in range(8):
            scores_ref[4 * q : 4 * q + 4, 128 * t : 128 * t + 128] = piece_all[q * 8 + t]

    scores = scores_ref[...] * (1.0 / math.sqrt(DOM * SLAB))
    power = jnp.exp(scores - jnp.max(scores, axis=0, keepdims=True))
    weights = (power / jnp.sum(power, axis=0, keepdims=True)).astype(BF16).astype(F32)
    coefficient_f32 = jnp.where(in_bin[None], weights[:, None, :], 0.0).reshape(PANELS, MEMBERS)
    coefficient_ref[...] = coefficient_f32.astype(BF16)
    tot_out[...] = dot_nt(jnp.ones((16, MEMBERS), BF16), coefficient_ref[...])[0:1]

    peers = [((cls // Y + dx) % 2) * Y + (cls + dy) % Y for dx, dy in STEPS]
    for peer in peers:
        send_to(tot_out, tot_in.at[cls], send.at[6], misc_recv.at[5], (peer, dom))
    tot_in[cls] = tot_out[...]
    for start in range(0, SLAB, 256):
        acc_out[:, :, start : start + 256] = (
            dot(coefficient_ref[...], x_ref[:, :, start : start + 256].reshape(MEMBERS, 256))
            .astype(BF16)
            .reshape(CLS, OWN, 256)
        )
    for peer in peers:
        send_to(acc_out.at[peer], acc_in.at[cls], send.at[5], misc_recv.at[4], (peer, dom))
    acc_in[cls] = acc_out[cls]

    taken(tot_in.at[pl.ds(0, CLS - 1)], misc_recv.at[5])
    total = jnp.sum(tot_in[...], axis=0)
    tot_col[...] = jnp.transpose(jnp.broadcast_to(total, (PANELS, 128)))
    own_total = tot_col[pl.ds(pl.multiple_of(cls * OWN, OWN), OWN), 0:1]
    taken(acc_in.at[pl.ds(0, CLS - 1)], misc_recv.at[4])
    out[...] = jnp.sum(acc_in[...].astype(F32), axis=0) / (own_total + 1.0)

    taken(c_ref.at[pl.ds(0, DOM - 1)], send.at[0])
    taken(r_ref.at[pl.ds(0, CLS - 1)], send.at[1])
    taken(x_ref.at[pl.ds(0, DOM - 1)], send.at[2])
    taken(piece_in.at[pl.ds(0, DOM - 1)], send.at[3])
    taken(piece_all.at[pl.ds(0, DOM - 1)], send.at[4])
    taken(acc_in.at[pl.ds(0, CLS - 1)], send.at[5])
    taken(tot_in.at[pl.ds(0, CLS - 1)], send.at[6])


def shards(particles, references, orient_bins, destinations, group_slots):
    hbm = pl.BlockSpec(memory_space=pltpu.HBM)
    out = pl.pallas_call(
        kernel,
        out_shape=jax.ShapeDtypeStruct((OWN, SLAB), F32),
        in_specs=[hbm] * 5,
        out_specs=pl.BlockSpec(memory_space=pltpu.VMEM),
        scratch_shapes=[
            pltpu.VMEM((DOM, ROWS, SLAB), BF16),
            pltpu.VMEM((ROWS, DOM * SLAB), BF16),
            pltpu.VMEM((3, 1, ROWS), jnp.int32),
            pltpu.VMEM((1, 128), jnp.int32),
            pltpu.VMEM((CLS, OWN, SLAB), BF16),
            pltpu.VMEM((DOM, 1, 128), jnp.int32),
            pltpu.VMEM((GROUPS, MEMBERS), BF16),
            pltpu.VMEM((MEMBERS, GROUPS), BF16),
            pltpu.VMEM((PANELS, MEMBERS), F32),
            pltpu.VMEM((PANELS, GROUPS), F32),
            pltpu.VMEM((DOM, 4, 128), F32),
            pltpu.VMEM((DOM, 4, 128), F32),
            pltpu.VMEM((DOM, 4, 128), F32),
            pltpu.VMEM((CLASSES, MEMBERS), F32),
            pltpu.VMEM((PANELS, MEMBERS), BF16),
            pltpu.VMEM((1, PANELS), F32),
            pltpu.VMEM((CLS, 1, PANELS), F32),
            pltpu.VMEM((PANELS, 128), F32),
            pltpu.VMEM((CLS, OWN, SLAB), BF16),
            pltpu.VMEM((CLS, OWN, SLAB), BF16),
            pltpu.SemaphoreType.DMA((CHUNKS,)),
            pltpu.SemaphoreType.DMA((6,)),
            pltpu.SemaphoreType.DMA((7,)),
            pltpu.SemaphoreType.DMA((5,)),
        ],
        compiler_params=pltpu.CompilerParams(
            collective_id=0, has_side_effects=True, vmem_limit_bytes=48 * 1024 * 1024
        ),
    )(
        *(
            pltpu.with_memory_space_constraint(value, pltpu.HBM)
            for value in (
                particles,
                references.reshape(OWN, DOM * SLAB),
                orient_bins.reshape(1, ROWS),
                destinations.reshape(1, ROWS),
                group_slots.reshape(1, ROWS),
            )
        )
    )
    return out.reshape(CLASSES // CLS, BINS, SLAB)


def solution(mesh):
    in_specs = (
        P(("cls", "dom"), None),
        P("cls", None, None),
        P(("cls", "dom")),
        P(("cls", "dom"), None),
        P(("cls", "dom")),
    )
    out_specs = P("cls", None, "dom")
    return jax.shard_map(shards, mesh=mesh, in_specs=in_specs, out_specs=out_specs, check_vma=False)
```

```python
import functools
import math

import jax
import jax.numpy as jnp
from jax import lax
from jax.experimental import pallas as pl
from jax.experimental.pallas import tpu as pltpu
from jax.sharding import PartitionSpec as P

MESH = pl.DeviceIdType.MESH
F32 = jnp.float32
BF16 = jnp.bfloat16

ROWS = 32
DOM = 32
CLS = 8
BINS = 8
CLASSES = 16
GROUPS = 256
MEMBERS = ROWS * DOM
SLAB = 1024
WIDTHS = (512, 384, 128)
STARTS = tuple(sum(WIDTHS[:c]) for c in range(len(WIDTHS)))
CHUNKS = len(WIDTHS)
WIDE = 128
PANELS = CLASSES * BINS
OWN = PANELS // CLS
Z = 8
Y = 4
STEPS = ((1, 2), (1, 1), (1, 3), (1, 0), (0, 2), (0, 1), (0, 3))

NT = (((1,), (1,)), ((), ()))


def dot(a, b):
    return jnp.dot(a, b, preferred_element_type=F32)


def dot_nt(a, b):
    return lax.dot_general(a, b, NT, preferred_element_type=F32)


def split(value, pieces):
    out = []
    for _ in range(pieces):
        piece = value.astype(BF16)
        out.append(piece)
        value = value - piece.astype(F32)
    return out


def dom_peer(i, dom):
    core, z, x = dom % 2, (dom // 2) % Z, dom // (2 * Z)
    j = i // 4
    step = 4 + (1 - 2 * (j % 2)) * ((j + 1) // 2)
    core = (core + 1 - i % 2) % 2
    x = (x + 1 - (i // 2) % 2) % 2
    z = (z + step) % Z
    return (x * Z + z) * 2 + core


def kernel(
    particles,
    references,
    orient_bins,
    destinations,
    group_slots,
    out,
    *scratch,
):
    (
        x_ref,
        rows,
        labels,
        codes,
        r_ref,
        c_ref,
        hot_t,
        hot,
        score_sum,
        energy_sum,
        piece_out,
        piece_in,
        piece_all,
        scores_ref,
        coefficient_ref,
        tot_out,
        tot_in,
        tot_col,
        acc_out,
        acc_in,
        x_recv,
        misc_recv,
        send,
        local,
    ) = scratch
    cls = lax.axis_index("cls")
    dom = lax.axis_index("dom")

    barrier = pltpu.get_barrier_semaphore()

    def greet_dom(i, carry):
        pl.semaphore_signal(barrier, inc=1, device_id=(cls, dom_peer(i, dom)), device_id_type=MESH)
        return carry

    def greet_cls(i, carry):
        pl.semaphore_signal(barrier, inc=1, device_id=((cls + i) % CLS, dom), device_id_type=MESH)
        return carry

    for i in range(DOM - 1):
        greet_dom(i, 0)
    lax.fori_loop(1, CLS, greet_cls, 0)

    slab_start = pl.multiple_of(dom * SLAB, SLAB)

    label_copies = [
        pltpu.make_async_copy(ref, labels.at[k], local.at[k])
        for k, ref in enumerate((destinations, group_slots, orient_bins))
    ]
    own_copies = [
        pltpu.make_async_copy(references.at[:, pl.ds(slab_start, SLAB)], r_ref.at[cls], local.at[3])
    ]
    staged = pltpu.make_async_copy(particles, rows, local.at[4])
    for copy in label_copies + own_copies + [staged]:
        copy.start()

    for copy in label_copies:
        copy.wait()
    own_code = (labels[0] * 8 + labels[1]) * BINS + labels[2]
    lane = lax.broadcasted_iota(jnp.int32, (1, 128), 1)
    four = jnp.concatenate([own_code] * 4, axis=1)
    codes[...] = jnp.where(lane // ROWS == dom % 4, four, 0)
    c_ref[dom] = codes[...]

    staged.wait()
    x_ref[dom] = rows[:, pl.ds(slab_start, SLAB)]
    pl.semaphore_wait(barrier, DOM - 1 + CLS - 1)

    def send_to(src, dst, sem_out, sem_in, device):
        pltpu.make_async_remote_copy(
            src_ref=src,
            dst_ref=dst,
            send_sem=sem_out,
            recv_sem=sem_in,
            device_id=device,
            device_id_type=MESH,
        ).start()

    def taken(ref, sem):
        pltpu.make_async_copy(ref, ref, sem).wait()

    def chunk_of(ref, chunk):
        return ref.at[pl.ds(0, DOM - 1), :, pl.ds(STARTS[chunk], WIDTHS[chunk])]

    def send_chunk(chunk):
        def body(i, carry):
            peer = dom_peer(i, dom)
            start = pl.multiple_of(peer * SLAB + STARTS[chunk], 128)
            send_to(
                rows.at[:, pl.ds(start, WIDTHS[chunk])],
                x_ref.at[dom, :, pl.ds(STARTS[chunk], WIDTHS[chunk])],
                send.at[2],
                x_recv.at[chunk],
                (cls, peer),
            )
            return carry

        for i in range(DOM - 1):
            body(i, 0)

    def send_codes(i, carry):
        send_to(codes, c_ref.at[dom], send.at[0], misc_recv.at[0], (cls, dom_peer(i, dom)))
        return carry

    def send_panels(i, carry):
        send_to(
            references.at[:, pl.ds(slab_start, SLAB)],
            r_ref.at[cls],
            send.at[1],
            misc_recv.at[1],
            ((cls + i) % CLS, dom),
        )
        return carry

    send_chunk(0)
    lax.fori_loop(0, DOM - 1, send_codes, 0)
    lax.fori_loop(1, CLS, send_panels, 0)
    for chunk in range(1, CHUNKS):
        send_chunk(chunk)

    taken(c_ref.at[pl.ds(0, DOM - 1)], misc_recv.at[0])
    code = jnp.sum(c_ref[...].reshape(8, 4, 128), axis=1)
    code_row = jnp.concatenate([code[t : t + 1] for t in range(8)], axis=1)
    group_row = code_row // BINS
    orient_row = code_row % BINS
    members = jnp.broadcast_to(group_row, (GROUPS, MEMBERS))
    hot_f32 = (lax.broadcasted_iota(jnp.int32, (GROUPS, MEMBERS), 0) == members).astype(F32)
    hot_t[...] = hot_f32.astype(BF16)
    counts = jnp.sum(hot_f32, axis=1, keepdims=True)
    group_col = jnp.transpose(jnp.broadcast_to(group_row.astype(F32), (128, MEMBERS)))
    lanes = lax.broadcasted_iota(jnp.int32, (MEMBERS, 128), 1).astype(F32)
    for half in range(GROUPS // 128):
        hot[:, 128 * half : 128 * half + 128] = (
            (group_col == lanes + float(128 * half)).astype(F32).astype(BF16)
        )
    score_sum[...] = jnp.zeros_like(score_sum)
    energy_sum[...] = jnp.zeros_like(energy_sum)

    taken(r_ref.at[pl.ds(0, CLS - 1)], misc_recv.at[1])
    for copy in own_copies:
        copy.wait()

    def whiten(part, carry):
        for chunk in range(CHUNKS):

            @pl.when(part == STARTS[chunk] // WIDE)
            def _():
                taken(chunk_of(x_ref, chunk), x_recv.at[chunk])

        lanes = pl.ds(pl.multiple_of(part * WIDE, WIDE), WIDE)
        values = x_ref[:, :, lanes].reshape(MEMBERS, WIDE).astype(F32)
        power = dot(hot_t[...], jnp.concatenate(split(values * values, 2), axis=1))
        inverse = (counts + 1.0) / (power[:, :WIDE] + power[:, WIDE:] + 1.0)
        parts = split(inverse, 3)
        spread = dot(hot[...], jnp.concatenate(parts[:2], axis=1))
        whitened = (values * (spread[:, :WIDE] + spread[:, WIDE:])).astype(BF16)
        x_ref[:, :, lanes] = whitened.reshape(DOM, ROWS, WIDE)
        panels = r_ref[:, :, lanes].reshape(PANELS, WIDE)
        score_sum[...] += dot_nt(panels, whitened)
        wide = panels.astype(F32)
        high, low = split(wide * wide, 2)
        squares = jnp.concatenate([high, high, high, low, low, low], axis=1)
        energy_sum[...] += dot_nt(squares, jnp.concatenate(parts + parts, axis=1))
        return carry

    lax.fori_loop(0, SLAB // WIDE, whiten, 0)

    spread_energy = jnp.zeros((PANELS, MEMBERS), F32)
    for part in split(energy_sum[...], 3):
        spread_energy += dot(part, hot_t[...])
    combined = (score_sum[...] - 0.5 * spread_energy).reshape(CLASSES, BINS, MEMBERS)
    bin_index = lax.broadcasted_iota(jnp.int32, (BINS, MEMBERS), 0)
    in_bin = bin_index == jnp.broadcast_to(orient_row, (BINS, MEMBERS))
    partial = jnp.sum(jnp.where(in_bin[None], combined, 0.0), axis=1)
    for q in range(4):
        for t in range(8):
            piece_out[q * 8 + t] = partial[4 * q : 4 * q + 4, 128 * t : 128 * t + 128]

    def send_piece(i, carry):
        peer = dom_peer(i, dom)
        send_to(piece_out.at[peer], piece_in.at[dom], send.at[3], misc_recv.at[2], (cls, peer))
        return carry

    for i in range(DOM - 1):
        send_piece(i, 0)
    piece_in[dom] = piece_out[dom]
    taken(piece_in.at[pl.ds(0, DOM - 1)], misc_recv.at[2])
    piece_all[dom] = jnp.sum(piece_in[...], axis=0)

    def send_sum(i, carry):
        peer = dom_peer(i, dom)
        send_to(piece_all.at[dom], piece_all.at[dom], send.at[4], misc_recv.at[3], (cls, peer))
        return carry

    for i in range(DOM - 1):
        send_sum(i, 0)
    taken(piece_all.at[pl.ds(0, DOM - 1)], misc_recv.at[3])
    for q in range(4):
        for t in range(8):
            scores_ref[4 * q : 4 * q + 4, 128 * t : 128 * t + 128] = piece_all[q * 8 + t]

    scores = scores_ref[...] * (1.0 / math.sqrt(DOM * SLAB))
    power = jnp.exp(scores - jnp.max(scores, axis=0, keepdims=True))
    weights = (power / jnp.sum(power, axis=0, keepdims=True)).astype(BF16).astype(F32)
    coefficient_f32 = jnp.where(in_bin[None], weights[:, None, :], 0.0).reshape(PANELS, MEMBERS)
    coefficient_ref[...] = coefficient_f32.astype(BF16)
    tot_out[...] = dot_nt(jnp.ones((16, MEMBERS), BF16), coefficient_ref[...])[0:1]

    peers = [((cls // Y + dx) % 2) * Y + (cls + dy) % Y for dx, dy in STEPS]
    for peer in peers:
        send_to(tot_out, tot_in.at[cls], send.at[6], misc_recv.at[5], (peer, dom))
    tot_in[cls] = tot_out[...]
    for start in range(0, SLAB, 256):
        acc_out[:, :, start : start + 256] = (
            dot(coefficient_ref[...], x_ref[:, :, start : start + 256].reshape(MEMBERS, 256))
            .astype(BF16)
            .reshape(CLS, OWN, 256)
        )
    for peer in peers:
        send_to(acc_out.at[peer], acc_in.at[cls], send.at[5], misc_recv.at[4], (peer, dom))
    acc_in[cls] = acc_out[cls]

    taken(tot_in.at[pl.ds(0, CLS - 1)], misc_recv.at[5])
    total = jnp.sum(tot_in[...], axis=0)
    tot_col[...] = jnp.transpose(jnp.broadcast_to(total, (PANELS, 128)))
    own_total = tot_col[pl.ds(pl.multiple_of(cls * OWN, OWN), OWN), 0:1]
    taken(acc_in.at[pl.ds(0, CLS - 1)], misc_recv.at[4])
    out[...] = jnp.sum(acc_in[...].astype(F32), axis=0) / (own_total + 1.0)

    taken(c_ref.at[pl.ds(0, DOM - 1)], send.at[0])
    taken(r_ref.at[pl.ds(0, CLS - 1)], send.at[1])
    taken(x_ref.at[pl.ds(0, DOM - 1)], send.at[2])
    taken(piece_in.at[pl.ds(0, DOM - 1)], send.at[3])
    taken(piece_all.at[pl.ds(0, DOM - 1)], send.at[4])
    taken(acc_in.at[pl.ds(0, CLS - 1)], send.at[5])
    taken(tot_in.at[pl.ds(0, CLS - 1)], send.at[6])


def shards(particles, references, orient_bins, destinations, group_slots):
    hbm = pl.BlockSpec(memory_space=pltpu.HBM)
    out = pl.pallas_call(
        kernel,
        out_shape=jax.ShapeDtypeStruct((OWN, SLAB), F32),
        in_specs=[hbm] * 5,
        out_specs=pl.BlockSpec(memory_space=pltpu.VMEM),
        scratch_shapes=[
            pltpu.VMEM((DOM, ROWS, SLAB), BF16),
            pltpu.VMEM((ROWS, DOM * SLAB), BF16),
            pltpu.VMEM((3, 1, ROWS), jnp.int32),
            pltpu.VMEM((1, 128), jnp.int32),
            pltpu.VMEM((CLS, OWN, SLAB), BF16),
            pltpu.VMEM((DOM, 1, 128), jnp.int32),
            pltpu.VMEM((GROUPS, MEMBERS), BF16),
            pltpu.VMEM((MEMBERS, GROUPS), BF16),
            pltpu.VMEM((PANELS, MEMBERS), F32),
            pltpu.VMEM((PANELS, GROUPS), F32),
            pltpu.VMEM((DOM, 4, 128), F32),
            pltpu.VMEM((DOM, 4, 128), F32),
            pltpu.VMEM((DOM, 4, 128), F32),
            pltpu.VMEM((CLASSES, MEMBERS), F32),
            pltpu.VMEM((PANELS, MEMBERS), BF16),
            pltpu.VMEM((1, PANELS), F32),
            pltpu.VMEM((CLS, 1, PANELS), F32),
            pltpu.VMEM((PANELS, 128), F32),
            pltpu.VMEM((CLS, OWN, SLAB), BF16),
            pltpu.VMEM((CLS, OWN, SLAB), BF16),
            pltpu.SemaphoreType.DMA((CHUNKS,)),
            pltpu.SemaphoreType.DMA((6,)),
            pltpu.SemaphoreType.DMA((7,)),
            pltpu.SemaphoreType.DMA((5,)),
        ],
        compiler_params=pltpu.CompilerParams(
            collective_id=0, has_side_effects=True, vmem_limit_bytes=48 * 1024 * 1024
        ),
    )(
        *(
            pltpu.with_memory_space_constraint(value, pltpu.HBM)
            for value in (
                particles,
                references.reshape(OWN, DOM * SLAB),
                orient_bins.reshape(1, ROWS),
                destinations.reshape(1, ROWS),
                group_slots.reshape(1, ROWS),
            )
        )
    )
    return out.reshape(CLASSES // CLS, BINS, SLAB)


def solution(mesh):
    in_specs = (
        P(("cls", "dom"), None),
        P("cls", None, None),
        P(("cls", "dom")),
        P(("cls", "dom"), None),
        P(("cls", "dom")),
    )
    out_specs = P("cls", None, "dom")
    return jax.shard_map(shards, mesh=mesh, in_specs=in_specs, out_specs=out_specs, check_vma=False)
```
